32 devices in a mesh: dp: 4 (over y, x), expert: 8 (over z, core).
Axes of the slice: x: 2, y: 2, z: 4, core: 2. Of those that a mesh axis runs over, the one named last changes fastest.
Arguments:
- tokens: bfloat16 [4096, 2048], P(('dp', 'expert')), may hold values from -6 to 6
- cotangent: bfloat16 [4096, 2048], P(('dp', 'expert')), may hold values from -3 to 3
- w_gate: bfloat16 [8, 2048, 768], P('expert'), may hold values from -0.125 to 0.125
- w_up: bfloat16 [8, 2048, 768], P('expert'), may hold values from -0.125 to 0.125
- w_down: bfloat16 [8, 768, 2048], P('expert'), may hold values from -0.21875 to 0.21875
- slot_rows: int32 [32, 8, 24], P(('dp', 'expert')), may hold values from 0 to 127, as said below
- slot_counts: int32 [32, 8], P(('dp', 'expert')), may hold values from 12 to 24, as said below
- slot_gates: float32 [32, 8, 24], P(('dp', 'expert')), may hold values from 0.1 to 1
- seq_lengths: int32 [32, 4], P(('dp', 'expert')), may hold values from 1 to 32, 96 in all within a row
- matching: int32 [8, 4], P('expert'), may hold values from 0 to 3, as said below
Outputs:
- output: bfloat16 [4096, 2048], P(('dp', 'expert'))
- grad_tokens: bfloat16 [4096, 2048], P(('dp', 'expert'))
- grad_w_gate: float32 [8, 2048, 768], P('expert', 'dp')
- grad_w_up: float32 [8, 2048, 768], P('expert', 'dp')
- grad_w_down: float32 [8, 768, 2048], P('expert', None, 'dp')
The draws below stay inside these ranges and needn't reach their ends.
Inputs may be any that keep to these rules, and one draw needn't show every extreme that they name: `slot_rows`: within one block the slots of one expert hold distinct rows, and no row is held by more than 8 slots of its block. `slot_counts`: in every draw one expert of the window, drawn anew, has 24 live slots in every block; the others have at least 12. matching[b, g] = g XOR k_b, with k_b of 1 to 3 common to all replicas at block position b, so partners are mutual; in every draw k_b = 2 at one or more positions. `seq_lengths`: the 4 lengths of each block sum to 96.
All inputs are finite; a program needn't handle non-finite values.
Results may differ from the reference program's by a relative error of at most 0.018.
Values may be sent and summed in bfloat16 or wider, within the bound.
No kernel may reach another device: no remote copies, remote signals or barrier semaphores. Data moves between devices by JAX's collectives and lax.ppermute only.
A program may use at most 128 MiB of HBM per device.

```python
import math
import jax
import jax.numpy as jnp
import numpy as np
from jax import lax

D = 2048
FF = 768
TOK_DEV = 128
B_DEV = 4
REPLICAS = 4
BLOCKS_REP = 8
SOURCES = 32
WIN = 8
SLOT = 32
CAP = 24
TOKENS = 4096


def route_tables(key):
    base = jax.random.fold_in(key, 17)
    perm_keys = jax.random.split(jax.random.fold_in(base, 1), SOURCES)

    def order_of(subkey):
        return jax.random.permutation(subkey, TOK_DEV)
    orders = jax.vmap(order_of)(perm_keys).astype(jnp.int32)
    offsets = (jnp.arange(WIN, dtype=jnp.int32)[:, None] * CAP + jnp.arange(CAP, dtype=jnp.int32)[None, :]) % TOK_DEV
    slot_table = orders[:, offsets]
    counts = jax.random.randint(jax.random.fold_in(base, 2), (SOURCES, WIN), CAP // 2, CAP + 1)
    busiest = jax.random.randint(jax.random.fold_in(base, 3), (), 0, WIN)
    counts = jnp.where(jnp.arange(WIN, dtype=jnp.int32)[None, :] == busiest, CAP, counts)
    return (slot_table.astype(jnp.int32), counts.astype(jnp.int32))


def draw_slot_rows(key, part):
    return route_tables(key)[0]


def draw_slot_counts(key, part):
    return route_tables(key)[1]


def draw_matching(key, part):
    pair_keys = jax.random.randint(jax.random.fold_in(key, 29), (BLOCKS_REP,), 1, REPLICAS).astype(jnp.int32)
    forced = jax.random.randint(jax.random.fold_in(key, 31), (), 0, BLOCKS_REP).astype(jnp.int32)
    pair_keys = jnp.where(jnp.arange(BLOCKS_REP, dtype=jnp.int32) == forced, REPLICAS // 2, pair_keys)
    replica_ids = jnp.arange(REPLICAS, dtype=jnp.int32)[None, :]
    return jnp.bitwise_xor(replica_ids, pair_keys[:, None]).astype(jnp.int32)


def steps_of(key, extent, shards, least, high):
    level = 1.0
    for position, shards_of in shards:
        heights = jax.random.uniform(jax.random.fold_in(jax.random.fold_in(key, 6), position), (shards_of,), jnp.float32, least / len(shards), high / len(shards))
        level = level * jnp.repeat(jnp.exp(heights), extent[position] // shards_of).reshape((-1,) + (1,) * (len(extent) - 1 - position))
    return level


def profile(amount, total, bound, skew):
    portions = [(1 << 20) // math.isqrt(rank ** skew) + 1 for rank in range(2, amount + 1)]
    spare, holding = total - bound - (amount - 1), [1] * (amount - 1)
    while spare > 0:
        free = [i for i in range(amount - 1) if holding[i] < bound]
        mass, budget = sum([portions[i] for i in free]), spare
        for i in free:
            extra = min(bound - holding[i], max(1, budget * portions[i] // mass), spare)
            holding[i] = holding[i] + extra
            spare = spare - extra
    return np.array([bound] + holding)


def uneven(key, number_of, total, reach, lean):
    if number_of == 2:
        one = jax.random.randint(key, (), max(1, total - reach), min(reach, total - 1) + 1)
        return jnp.stack([one, total - one])
    tallies = jnp.asarray(profile(number_of, total, reach, lean), jnp.int32)
    pairs = (number_of - 1) // 2
    source_of, receiver = tallies[1:1 + 2 * pairs:2], tallies[2:2 + 2 * pairs:2]
    room = jnp.minimum(source_of - 1, reach - receiver)
    passed = jax.random.randint(jax.random.fold_in(key, 1), (pairs,), 0, 1 << 20) % (room + 1)
    tallies = tallies.at[1:1 + 2 * pairs:2].set(source_of - passed).at[2:2 + 2 * pairs:2].set(receiver + passed)
    return tallies[jax.random.permutation(jax.random.fold_in(key, 2), number_of)]


def gaussian(rng, shape, scale, reach, cuts=(), kind=jnp.bfloat16):
    values = jax.random.normal(rng, shape, jnp.float32) * scale
    if len(cuts) > 0:
        values = steps_of(rng, shape, cuts, -0.22, 0.18) * values
    return jnp.clip(values, min=-reach, max=reach).astype(kind)


def setup_inputs(seed: int = 0) -> dict:
    streams_of = jax.random.split(jax.random.key(seed), 11)
    tokens = gaussian(streams_of[0], (TOKENS, D), 1.0, 6.0, ((0, 32),))
    cotangent = gaussian(streams_of[1], (TOKENS, D), 0.5, 3.0, ((0, 32),))
    w_gate = gaussian(streams_of[2], (WIN, D, FF), D ** -0.5, 0.125, ((0, 8),))
    w_up = gaussian(streams_of[3], (WIN, D, FF), D ** -0.5, 0.125, ((0, 8),))
    w_down = gaussian(streams_of[4], (WIN, FF, D), FF ** -0.5, 0.21875, ((0, 8),))
    slot_rows = draw_slot_rows(jax.random.fold_in(streams_of[10], 71), 0)
    slot_counts = draw_slot_counts(jax.random.fold_in(streams_of[10], 71), 0)
    slot_gates = jnp.clip(jnp.exp(math.log(1.0) - 2.3025851 * jax.random.uniform(streams_of[7], (SOURCES, WIN, CAP), jnp.float32) ** steps_of(streams_of[7], (SOURCES, WIN, CAP), ((0, 32),), -0.2, 0.2)), 0.1, 1.0)
    seq_lengths = jax.vmap(lambda own: uneven(own, B_DEV, 3 * TOK_DEV // 4, SLOT, 0))(jax.random.split(streams_of[8], SOURCES)).reshape((SOURCES, B_DEV)).astype(jnp.int32)
    matching = draw_matching(jax.random.fold_in(streams_of[10], 71), 0)
    return dict(tokens=tokens, cotangent=cotangent, w_gate=w_gate, w_up=w_up, w_down=w_down, slot_rows=slot_rows, slot_counts=slot_counts, slot_gates=slot_gates, seq_lengths=seq_lengths, matching=matching)


def swap_halves(stacked, matching):
    half_size = stacked.shape[2] // 2
    partner_rows = jnp.transpose(matching, (1, 0))
    position_ids = jnp.arange(stacked.shape[1], dtype=jnp.int32)[None, :]
    moved = stacked[partner_rows, position_ids]
    return jnp.concatenate([stacked[:, :, :half_size], moved[:, :, half_size:]], axis=2)


def reference(tokens, cotangent, w_gate, w_up, w_down, slot_rows, slot_counts, slot_gates, seq_lengths, matching):
    blocks = tokens.reshape(REPLICAS, BLOCKS_REP, TOK_DEV, D)
    row_index = jnp.arange(TOK_DEV, dtype=jnp.int32)
    lengths_rows = seq_lengths[:, row_index // SLOT]
    valid_rows = (row_index[None, :] % SLOT < lengths_rows).astype(jnp.float32)
    valid_rows = valid_rows.reshape(REPLICAS, BLOCKS_REP, TOK_DEV)
    shuffled = swap_halves(blocks, matching).reshape(SOURCES, TOK_DEV, D)
    valid_swapped = swap_halves(valid_rows, matching).reshape(SOURCES, TOK_DEV)
    slot_live = (jnp.arange(CAP, dtype=jnp.int32)[None, None, :] < slot_counts[:, :, None]).astype(jnp.float32)
    valid_at = jnp.take_along_axis(valid_swapped, slot_rows.reshape(SOURCES, WIN * CAP), axis=1)
    live_gate = slot_gates * slot_live * valid_at.reshape(SOURCES, WIN, CAP)
    cot_blocks = cotangent.reshape(SOURCES, TOK_DEV, D)
    source_ids = jnp.arange(SOURCES, dtype=jnp.int32)[:, None]

    def per_expert(totals, inputs):
        gate_matrix, up_matrix, down_matrix, rows_expert, live_expert = inputs
        picked = shuffled[source_ids, rows_expert].reshape(SOURCES * CAP, D)
        pre_gate = jnp.dot(picked, gate_matrix, preferred_element_type=jnp.float32)
        pre_up = jnp.dot(picked, up_matrix, preferred_element_type=jnp.float32)
        sigmoid_gate = jax.nn.sigmoid(pre_gate)
        silu_gate = pre_gate * sigmoid_gate
        hidden = (silu_gate * pre_up).astype(jnp.bfloat16)
        expert_out = jnp.dot(hidden, down_matrix, preferred_element_type=jnp.float32).astype(jnp.bfloat16)
        live_flat = live_expert.reshape(SOURCES * CAP, 1)
        cot_rows = cot_blocks[source_ids, rows_expert].reshape(SOURCES * CAP, D)
        weighted = (live_flat * cot_rows.astype(jnp.float32)).astype(jnp.bfloat16)
        grad_hidden = jnp.dot(weighted, down_matrix.T, preferred_element_type=jnp.float32)
        grad_gate = (grad_hidden * pre_up * sigmoid_gate * (1.0 + pre_gate * (1.0 - sigmoid_gate))).astype(jnp.bfloat16)
        grad_up = (grad_hidden * silu_gate).astype(jnp.bfloat16)
        token_rows = (jnp.dot(grad_gate, gate_matrix.T, preferred_element_type=jnp.float32)
                      + jnp.dot(grad_up, up_matrix.T, preferred_element_type=jnp.float32)).astype(jnp.bfloat16)
        out_total, grad_total = totals
        out_total = out_total.at[source_ids, rows_expert].add(
            (live_flat * expert_out.astype(jnp.float32)).reshape(SOURCES, CAP, D))
        grad_total = grad_total.at[source_ids, rows_expert].add(
            token_rows.astype(jnp.float32).reshape(SOURCES, CAP, D))
        weight_grads = (jnp.dot(picked.T, grad_gate, preferred_element_type=jnp.float32),
                        jnp.dot(picked.T, grad_up, preferred_element_type=jnp.float32),
                        jnp.dot(hidden.T, weighted, preferred_element_type=jnp.float32))
        return (out_total, grad_total), weight_grads

    empty_total = jnp.zeros((SOURCES, TOK_DEV, D), jnp.float32)
    (out_total, grad_total), (grad_w_gate, grad_w_up, grad_w_down) = lax.scan(
        per_expert, (empty_total, empty_total),
        (w_gate, w_up, w_down, jnp.transpose(slot_rows, (1, 0, 2)), jnp.transpose(live_gate, (1, 0, 2))))
    output = out_total.astype(jnp.bfloat16).reshape(TOKENS, D)
    grad_shuffled = grad_total.astype(jnp.bfloat16).reshape(REPLICAS, BLOCKS_REP, TOK_DEV, D)
    grad_tokens = swap_halves(grad_shuffled, matching).reshape(TOKENS, D)
    return (output, grad_tokens, grad_w_gate, grad_w_up, grad_w_down)
```

```python
import functools

import jax
import jax.numpy as jnp
from jax import lax
from jax.experimental import pallas as pl
from jax.experimental.pallas import tpu as pltpu
from jax.sharding import PartitionSpec as P

F32 = jnp.float32
BF16 = jnp.bfloat16
VMEM = pltpu.VMEM
WHOLE = pl.BlockSpec(memory_space=pltpu.VMEM)
SCALARS = pl.BlockSpec(memory_space=pltpu.SMEM)
TILE = 256
LIMIT = 56 * 1024 * 1024


def params():
    return pltpu.CompilerParams(vmem_limit_bytes=LIMIT)


def cost(flops, bytes_accessed):
    return pl.CostEstimate(flops=int(flops), bytes_accessed=int(bytes_accessed), transcendentals=0)


def xor_permute(array, axis, key):
    size = lax.axis_size(axis)
    return lax.ppermute(array, axis, [(i, i ^ key) for i in range(size)])


def column_of(row, length):
    diagonal = lax.broadcasted_iota(jnp.int32, (length, length), 0) == lax.broadcasted_iota(
        jnp.int32, (length, length), 1
    )
    spread = jnp.where(diagonal, jnp.broadcast_to(row.astype(F32), (length, length)), 0.0)
    return jnp.sum(spread, axis=1, keepdims=True)


def relative_columns(table_ref, me, window, capacity):
    return jnp.concatenate(
        [column_of(table_ref[0, pl.ds(me ^ d, 1), :], capacity) for d in range(window)], axis=0
    )


def slot_onehot(rows_ref, me, window, capacity, tok_dev):
    index = relative_columns(rows_ref, me, window, capacity).astype(jnp.int32)
    lanes = lax.broadcasted_iota(jnp.int32, (window * capacity, tok_dev), 1)
    return lanes == index


def counted_gates(gates_ref, counts_ref, me, window, capacity):
    parts = []
    for d in range(window):
        slot = lax.broadcasted_iota(jnp.int32, (1, capacity), 1)
        gate = gates_ref[0, pl.ds(me ^ d, 1), :]
        gate = jnp.where(slot < counts_ref[0, me ^ d], gate, 0.0)
        parts.append(column_of(gate, capacity))
    return jnp.concatenate(parts, axis=0)


def keep_valid(values, lengths_ref, first_slot, slot_len):
    rows = lax.broadcasted_iota(jnp.int32, values.shape, 0)
    limit = jnp.zeros(values.shape, jnp.int32)
    for slot in range(values.shape[0] // slot_len):
        limit = jnp.where(
            rows // slot_len == slot, slot * slot_len + lengths_ref[0, first_slot + slot], limit
        )
    return jnp.where(rows < limit, values.astype(F32), 0.0).astype(values.dtype)


def prepare_kernel(sizes, rows_ref, gates_ref, counts_ref, lengths_ref, cot_ref, tok_ref, *outs):
    window, capacity, tok_dev, slot_len = sizes
    me = lax.axis_index("expert")
    moved_ref, outs = outs[0], outs[1:]
    half = tok_dev // 2
    moved_ref[...] = keep_valid(tok_ref[...], lengths_ref, half // slot_len, slot_len)
    hit = slot_onehot(rows_ref, me, window, capacity, tok_dev).astype(BF16)
    gate = counted_gates(gates_ref, counts_ref, me, window, capacity)
    picked = jnp.dot(hit, cot_ref[...], preferred_element_type=F32)
    weighted = (gate * picked).astype(BF16)
    for z, out in enumerate(outs):
        out[...] = weighted[z * 2 * capacity : (z + 1) * 2 * capacity]


def prepare(slot_rows, slot_gates, slot_counts, seq_lengths, cotangent, tokens):
    tok_dev, width = tokens.shape
    window, capacity = slot_rows.shape[1:]
    half = tok_dev // 2
    slot_len = tok_dev // seq_lengths.shape[1]
    sizes = (window, capacity, tok_dev, slot_len)
    return pl.pallas_call(
        functools.partial(prepare_kernel, sizes),
        grid=(1,),
        out_shape=[jax.ShapeDtypeStruct((half, width), BF16)]
        + [jax.ShapeDtypeStruct((2 * capacity, width), BF16)] * (window // 2),
        in_specs=[
            pl.BlockSpec(slot_rows.shape, lambda i: (0, 0, 0)),
            pl.BlockSpec(slot_gates.shape, lambda i: (0, 0, 0)),
            SCALARS,
            SCALARS,
            pl.BlockSpec(cotangent.shape, lambda i: (0, 0)),
            pl.BlockSpec((half, width), lambda i: (1, 0)),
        ],
        out_specs=[pl.BlockSpec((half, width), lambda i: (0, 0))]
        + [pl.BlockSpec((2 * capacity, width), lambda i: (0, 0))] * (window // 2),
        compiler_params=params(),
        cost_estimate=cost(2 * window * capacity * tok_dev * width, 5 * tok_dev * width),
        name="prepare",
    )(slot_rows, slot_gates, slot_counts, seq_lengths, cotangent, tokens)


def chosen(key, refs):
    value = refs[0][...].astype(F32)
    for i in range(1, len(refs)):
        value = jnp.where(key == i + 1, refs[i][...].astype(F32), value)
    return value.astype(BF16)


def pick_kernel(sizes, rows_ref, lengths_ref, matching_ref, tok_ref, *refs):
    window, capacity, tok_dev, slot_len, partners = sizes
    me = lax.axis_index("expert")
    arrived, outs = refs[:partners], refs[partners:]
    key = matching_ref[0, 0]
    low = keep_valid(tok_ref[...], lengths_ref, 0, slot_len)
    shuffled = jnp.concatenate([low, chosen(key, arrived)], axis=0)
    hit = slot_onehot(rows_ref, me, window, capacity, tok_dev).astype(BF16)
    picked = jnp.dot(hit, shuffled, preferred_element_type=F32).astype(BF16)
    for z, out in enumerate(outs):
        out[...] = picked[z * 2 * capacity : (z + 1) * 2 * capacity]


def pick(slot_rows, seq_lengths, matching, tokens, arrived):
    tok_dev, width = tokens.shape
    window, capacity = slot_rows.shape[1:]
    half = tok_dev // 2
    slot_len = tok_dev // seq_lengths.shape[1]
    sizes = (window, capacity, tok_dev, slot_len, len(arrived))
    return pl.pallas_call(
        functools.partial(pick_kernel, sizes),
        grid=(1,),
        out_shape=[jax.ShapeDtypeStruct((2 * capacity, width), BF16)] * (window // 2),
        in_specs=[
            pl.BlockSpec(slot_rows.shape, lambda i: (0, 0, 0)),
            SCALARS,
            SCALARS,
            pl.BlockSpec((half, width), lambda i: (0, 0)),
        ]
        + [pl.BlockSpec((half, width), lambda i: (0, 0))] * len(arrived),
        out_specs=[pl.BlockSpec((2 * capacity, width), lambda i: (0, 0))] * (window // 2),
        compiler_params=params(),
        cost_estimate=cost(2 * window * capacity * tok_dev * width, 5 * tok_dev * width),
        name="pick",
    )(slot_rows, seq_lengths, matching, tokens, *arrived)


def joined(direct, crossed, capacity):
    rows = lax.broadcasted_iota(jnp.int32, direct.shape, 0)
    return jnp.where(rows < capacity, direct[...].astype(F32), crossed[...].astype(F32)).astype(BF16)


def expert_kernel(sizes, *refs):
    count, capacity, steps, replicas, share = sizes
    x_refs, w_refs = refs[: 2 * count], refs[2 * count : 4 * count]
    gate_ref, up_ref, down_ref = refs[4 * count : 4 * count + 3]
    outs = refs[4 * count + 3 :]
    tok_refs, out_refs = outs[:count], outs[count : 2 * count]
    slice_refs = outs[2 * count : 2 * count + replicas]
    acts_ref, x_all, w_all, tok_sum, out_sum = outs[2 * count + replicas :]
    step = pl.program_id(0)
    pair = 2 * capacity

    @pl.when(step == 0)
    def _():
        for z in range(count):
            rows = slice(z * pair, (z + 1) * pair)
            x_all[rows, :] = joined(x_refs[2 * z], x_refs[2 * z + 1], capacity)
            w_all[rows, :] = joined(w_refs[2 * z], w_refs[2 * z + 1], capacity)
        me = lax.axis_index("dp")
        for j in range(replicas):
            columns = pl.ds(pl.multiple_of((me ^ j) * share, share), share)
            slice_refs[j][:, :share] = x_all[:, columns]
            slice_refs[j][:, share:] = w_all[:, columns]

    x, w = x_all[...], w_all[...]
    w_gate, w_up, w_down = gate_ref[0], up_ref[0], down_ref[0]
    pre_gate = jnp.dot(x, w_gate, preferred_element_type=F32)
    pre_up = jnp.dot(x, w_up, preferred_element_type=F32)
    turned = (((1,), (1,)), ((), ()))
    grad_hidden = lax.dot_general(w, w_down, turned, preferred_element_type=F32)
    sig = jax.nn.sigmoid(pre_gate)
    silu = pre_gate * sig
    hidden = (silu * pre_up).astype(BF16)
    grad_gate = (grad_hidden * pre_up * sig * (1.0 + pre_gate * (1.0 - sig))).astype(BF16)
    grad_up = (grad_hidden * silu).astype(BF16)
    acts_ref[...] = jnp.concatenate([hidden, grad_gate, grad_up], axis=1)
    tok = lax.dot_general(grad_gate, w_gate, turned, preferred_element_type=F32)
    tok += lax.dot_general(grad_up, w_up, turned, preferred_element_type=F32)
    out = jnp.dot(hidden, w_down, preferred_element_type=F32)

    @pl.when(step == 0)
    def _():
        tok_sum[...] = tok
        out_sum[...] = out

    @pl.when(step > 0)
    def _():
        tok_sum[...] += tok
        out_sum[...] += out

    @pl.when(step == steps - 1)
    def _():
        for z in range(count):
            rows = slice(z * pair, (z + 1) * pair)
            tok_refs[z][...] = tok_sum[rows, :].astype(BF16)
            out_refs[z][...] = out_sum[rows, :].astype(BF16)


def expert(x_pairs, w_pairs, w_gate, w_up, w_down, capacity):
    count = len(x_pairs)
    pair, width = x_pairs[0][0].shape
    hidden_units = w_gate.shape[2]
    rows = count * pair
    replicas = lax.axis_size("dp")
    share = width // replicas
    tile = TILE
    steps = hidden_units // tile
    sizes = (count, capacity, steps, replicas, share)
    flat = [a for p in x_pairs for a in p] + [a for p in w_pairs for a in p]
    fixed = lambda f: (0, 0)
    block = jax.ShapeDtypeStruct((pair, width), BF16)
    acts = jax.ShapeDtypeStruct((rows, 3 * hidden_units), BF16)
    results = pl.pallas_call(
        functools.partial(expert_kernel, sizes),
        grid=(steps,),
        out_shape=[block] * (2 * count)
        + [jax.ShapeDtypeStruct((rows, 2 * share), BF16)] * replicas
        + [acts],
        in_specs=[pl.BlockSpec((pair, width), fixed)] * (4 * count)
        + [
            pl.BlockSpec((1, width, tile), lambda f: (0, 0, f)),
            pl.BlockSpec((1, width, tile), lambda f: (0, 0, f)),
            pl.BlockSpec((1, tile, width), lambda f: (0, f, 0)),
        ],
        out_specs=[pl.BlockSpec((pair, width), fixed)] * (2 * count)
        + [pl.BlockSpec((rows, 2 * share), fixed)] * replicas
        + [pl.BlockSpec((rows, 3 * tile), lambda f: (0, f))],
        scratch_shapes=[
            VMEM((rows, width), BF16),
            VMEM((rows, width), BF16),
            VMEM((rows, width), F32),
            VMEM((rows, width), F32),
        ],
        compiler_params=params(),
        cost_estimate=cost(
            12 * rows * width * hidden_units, 6 * width * hidden_units + 10 * rows * width
        ),
        name="expert",
    )(*flat, w_gate, w_up, w_down)
    token_rows, expert_out = results[:count], results[count : 2 * count]
    slices = results[2 * count : 2 * count + replicas]
    return token_rows, expert_out, slices, results[-1]


def weight_kernel(sizes, *refs):
    parts, share, tile = sizes
    slices, acts = refs[:parts], refs[parts : 2 * parts]
    gate_out, up_out, down_out = refs[2 * parts :]
    across = (((0,), (0,)), ((), ()))
    x = jnp.concatenate([s[:, :share] for s in slices], axis=0)
    w = jnp.concatenate([s[:, share:] for s in slices], axis=0)
    hidden = jnp.concatenate([a[:, :tile] for a in acts], axis=0)
    grad_gate = jnp.concatenate([a[:, tile : 2 * tile] for a in acts], axis=0)
    grad_up = jnp.concatenate([a[:, 2 * tile :] for a in acts], axis=0)
    gate_out[0] = lax.dot_general(x, grad_gate, across, preferred_element_type=F32)
    up_out[0] = lax.dot_general(x, grad_up, across, preferred_element_type=F32)
    down_out[0] = lax.dot_general(hidden, w, across, preferred_element_type=F32)


def weight_grads(slices, acts):
    parts = len(slices)
    share = slices[0].shape[1] // 2
    hidden_units = acts[0].shape[1] // 3
    tile = TILE
    rows = sum(s.shape[0] for s in slices)
    return pl.pallas_call(
        functools.partial(weight_kernel, (parts, share, tile)),
        grid=(hidden_units // tile,),
        out_shape=[
            jax.ShapeDtypeStruct((1, share, hidden_units), F32),
            jax.ShapeDtypeStruct((1, share, hidden_units), F32),
            jax.ShapeDtypeStruct((1, hidden_units, share), F32),
        ],
        in_specs=[pl.BlockSpec(s.shape, lambda f: (0, 0)) for s in slices]
        + [pl.BlockSpec((a.shape[0], 3 * tile), lambda f: (0, f)) for a in acts],
        out_specs=[
            pl.BlockSpec((1, share, tile), lambda f: (0, 0, f)),
            pl.BlockSpec((1, share, tile), lambda f: (0, 0, f)),
            pl.BlockSpec((1, tile, share), lambda f: (0, f, 0)),
        ],
        compiler_params=params(),
        cost_estimate=cost(6 * rows * share * hidden_units, 12 * share * hidden_units),
        name="weight_grads",
    )(*slices, *acts)


def assemble(refs, capacity):
    return jnp.concatenate(
        [joined(refs[2 * z], refs[2 * z + 1], capacity) for z in range(len(refs) // 2)], axis=0
    )


def output_kernel(sizes, rows_ref, gates_ref, counts_ref, *refs):
    window, capacity, tok_dev = sizes
    me = lax.axis_index("expert")
    hit = slot_onehot(rows_ref, me, window, capacity, tok_dev)
    gate = counted_gates(gates_ref, counts_ref, me, window, capacity)
    table = jnp.where(hit, jnp.broadcast_to(gate, hit.shape), 0.0)
    high = table.astype(BF16)
    low = (table - high.astype(F32)).astype(BF16)
    rows = assemble(refs[:-1], capacity)
    across = (((0,), (0,)), ((), ()))
    total = lax.dot_general(high, rows, across, preferred_element_type=F32)
    total += lax.dot_general(low, rows, across, preferred_element_type=F32)
    refs[-1][...] = total.astype(BF16)


def combine_output(slot_rows, slot_gates, slot_counts, pairs, tok_dev):
    window, capacity = slot_rows.shape[1:]
    flat = [a for p in pairs for a in p]
    width = flat[0].shape[1]
    return pl.pallas_call(
        functools.partial(output_kernel, (window, capacity, tok_dev)),
        out_shape=jax.ShapeDtypeStruct((tok_dev, width), BF16),
        in_specs=[WHOLE, WHOLE, SCALARS] + [WHOLE] * len(flat),
        out_specs=WHOLE,
        compiler_params=params(),
        cost_estimate=cost(4 * window * capacity * tok_dev * width, 6 * tok_dev * width),
        name="combine_output",
    )(slot_rows, slot_gates, slot_counts, *flat)


def grads_kernel(sizes, rows_ref, *refs):
    window, capacity, tok_dev = sizes
    me = lax.axis_index("expert")
    hit = slot_onehot(rows_ref, me, window, capacity, tok_dev).astype(BF16)
    rows = assemble(refs[:-2], capacity)
    across = (((0,), (0,)), ((), ()))
    total = lax.dot_general(hit, rows, across, preferred_element_type=F32).astype(BF16)
    refs[-2][...] = total[: tok_dev // 2]
    refs[-1][...] = total[tok_dev // 2 :]


def combine_grads(slot_rows, pairs, tok_dev):
    window, capacity = slot_rows.shape[1:]
    flat = [a for p in pairs for a in p]
    width = flat[0].shape[1]
    half = jax.ShapeDtypeStruct((tok_dev // 2, width), BF16)
    return pl.pallas_call(
        functools.partial(grads_kernel, (window, capacity, tok_dev)),
        out_shape=[half, half],
        in_specs=[WHOLE] * (1 + len(flat)),
        out_specs=[WHOLE, WHOLE],
        compiler_params=params(),
        cost_estimate=cost(2 * window * capacity * tok_dev * width, 6 * tok_dev * width),
        name="combine_grads",
    )(slot_rows, *flat)


def finish_kernel(matching_ref, low_ref, *refs):
    out_ref = refs[-1]
    half = low_ref.shape[0]
    out_ref[:half] = low_ref[...]
    out_ref[half:] = chosen(matching_ref[0, 0], refs[:-1])


def finish(matching, low, arrived):
    half, width = low.shape
    return pl.pallas_call(
        finish_kernel,
        out_shape=jax.ShapeDtypeStruct((2 * half, width), BF16),
        in_specs=[SCALARS, WHOLE] + [WHOLE] * len(arrived),
        out_specs=WHOLE,
        compiler_params=params(),
        cost_estimate=cost(0, 10 * half * width),
        name="finish",
    )(matching, low, *arrived)


def exchange(blocks):
    direct = {0: blocks[0]}
    for z in range(len(blocks) - 1, 0, -1):
        direct[z] = xor_permute(blocks[z], "expert", 2 * z)
    return [(direct[z], xor_permute(direct[z], "expert", 1)) for z in range(len(blocks))]


def spread(array):
    return [array] + [xor_permute(array, "dp", j) for j in range(1, lax.axis_size("dp"))]


def per_device(
    tokens,
    cotangent,
    w_gate,
    w_up,
    w_down,
    slot_rows,
    slot_counts,
    slot_gates,
    seq_lengths,
    matching,
):
    tok_dev = tokens.shape[0]
    capacity = slot_rows.shape[2]
    replicas = lax.axis_size("dp")
    moved, *weighted = prepare(slot_rows, slot_gates, slot_counts, seq_lengths, cotangent, tokens)
    w_pairs = exchange(weighted)
    arrived = spread(moved)[1:]
    picked = pick(slot_rows, seq_lengths, matching, tokens, arrived)
    x_pairs = exchange(picked)
    token_rows, expert_out, slices, acts = expert(x_pairs, w_pairs, w_gate, w_up, w_down, capacity)
    tok_pairs = exchange(token_rows)
    out_pairs = exchange(expert_out)
    all_slices = [slices[0]] + [xor_permute(slices[j], "dp", j) for j in range(1, replicas)]
    all_acts = spread(acts)
    low, high = combine_grads(slot_rows, tok_pairs, tok_dev)
    grad_tokens = finish(matching, low, spread(high)[1:])
    grads = weight_grads(all_slices, all_acts)
    output = combine_output(slot_rows, slot_gates, slot_counts, out_pairs, tok_dev)
    return (output, grad_tokens, *grads)


def solution(mesh):
    return jax.shard_map(
        per_device,
        mesh=mesh,
        in_specs=(
            P(("dp", "expert"), None),
            P(("dp", "expert"), None),
            P("expert", None, None),
            P("expert", None, None),
            P("expert", None, None),
            P(("dp", "expert"), None, None),
            P(("dp", "expert"), None),
            P(("dp", "expert"), None, None),
            P(("dp", "expert"), None),
            P("expert", None),
        ),
        out_specs=(
            P(("dp", "expert"), None),
            P(("dp", "expert"), None),
            P("expert", "dp", None),
            P("expert", "dp", None),
            P("expert", None, "dp"),
        ),
        check_vma=False,
    )
```

```python
import functools

import jax
import jax.numpy as jnp
from jax import lax
from jax.experimental import pallas as pl
from jax.experimental.pallas import tpu as pltpu
from jax.sharding import PartitionSpec as P

F32 = jnp.float32
BF16 = jnp.bfloat16
VMEM = pltpu.VMEM
WHOLE = pl.BlockSpec(memory_space=pltpu.VMEM)
TILE = 256
MIB = 1024 * 1024


def params(mib):
    return pltpu.CompilerParams(vmem_limit_bytes=mib * MIB)


def in_hbm(*arrays):
    return [pltpu.with_memory_space_constraint(a, pltpu.HBM) for a in arrays]


def cost(flops, bytes_accessed):
    return pl.CostEstimate(flops=int(flops), bytes_accessed=int(bytes_accessed), transcendentals=0)


def xor_permute(array, axis, key):
    size = lax.axis_size(axis)
    return lax.ppermute(array, axis, [(i, i ^ key) for i in range(size)])


def column_of(row, length):
    diagonal = lax.broadcasted_iota(jnp.int32, (length, length), 0) == lax.broadcasted_iota(
        jnp.int32, (length, length), 1
    )
    spread = jnp.where(diagonal, jnp.broadcast_to(row.astype(F32), (length, length)), 0.0)
    return jnp.sum(spread, axis=1, keepdims=True)


def table_columns(table, order):
    return jnp.concatenate([column_of(row, row.shape[1]) for row in (table(e) for e in order)], axis=0)


def keep_valid(values, lengths, first_slot, slot_len):
    rows = lax.broadcasted_iota(jnp.int32, values.shape, 0)
    limit = jnp.zeros(values.shape, jnp.int32)
    for slot in range(values.shape[0] // slot_len):
        used = lengths[:, first_slot + slot : first_slot + slot + 1]
        limit = jnp.where(rows // slot_len == slot, slot * slot_len + used, limit)
    return jnp.where(rows < limit, values.astype(F32), 0.0).astype(values.dtype)


def prepare_kernel(sizes, *refs):
    window, capacity, tok_dev, slot_len = sizes
    sources, outs, held, sems = refs[:7], refs[7:14], refs[14:21], refs[21]
    copies = [
        pltpu.make_async_copy(source, place, sems.at[i])
        for i, (source, place) in enumerate(zip(sources, held))
    ]
    for copy in copies:
        copy.start()
    for copy in copies:
        copy.wait()
    rows_ref, gates_ref, counts_ref, lengths_ref, matching_ref, tok_ref, cot_ref = held
    moved_ref, low_ref, weighted_ref, hit_ref, high_ref, fine_ref, key_ref = outs
    me = lax.axis_index("expert")
    half = tok_dev // 2
    lengths = lengths_ref[...]
    moved_ref[...] = keep_valid(tok_ref[half:, :], lengths, half // slot_len, slot_len)
    low_ref[...] = keep_valid(tok_ref[:half, :], lengths, 0, slot_len)
    key_ref[...] = jnp.broadcast_to(matching_ref[:, :1], key_ref.shape)
    lanes = lax.broadcasted_iota(jnp.int32, (window * capacity, tok_dev), 1)
    row_of = lambda e: rows_ref[0, pl.ds(e, 1), :]
    hit_ref[...] = (
        lanes == table_columns(row_of, [me ^ d for d in range(window)]).astype(jnp.int32)
    ).astype(BF16)

    def gate_of(e):
        slot = lax.broadcasted_iota(jnp.int32, (1, capacity), 1)
        counted = slot < counts_ref[:, e : e + 1]
        return jnp.where(counted, gates_ref[0, e : e + 1, :], 0.0)

    gate = table_columns(gate_of, range(window))
    hit = lanes == table_columns(row_of, range(window)).astype(jnp.int32)
    table = jnp.where(hit, jnp.broadcast_to(gate, hit.shape), 0.0)
    high = table.astype(BF16)
    high_ref[...] = high
    fine_ref[...] = (table - high.astype(F32)).astype(BF16)
    picked = jnp.dot(hit.astype(BF16), cot_ref[...], preferred_element_type=F32)
    weighted = gate * picked
    for e in range(window):
        weighted_ref[e] = weighted[e * capacity : (e + 1) * capacity].astype(BF16)


def prepare(slot_rows, slot_gates, slot_counts, seq_lengths, matching, tokens, cotangent):
    tok_dev, width = tokens.shape
    window, capacity = slot_rows.shape[1:]
    half = tok_dev // 2
    slot_len = tok_dev // seq_lengths.shape[1]
    sources = (slot_rows, slot_gates, slot_counts, seq_lengths, matching, tokens, cotangent)
    table = jax.ShapeDtypeStruct((window * capacity, tok_dev), BF16)
    return pl.pallas_call(
        functools.partial(prepare_kernel, (window, capacity, tok_dev, slot_len)),
        out_shape=[
            jax.ShapeDtypeStruct((half, width), BF16),
            jax.ShapeDtypeStruct((half, width), BF16),
            jax.ShapeDtypeStruct((window, capacity, width), BF16),
            table,
            table,
            table,
            jax.ShapeDtypeStruct((8, 128), jnp.int32),
        ],
        in_specs=[pl.BlockSpec(memory_space=pltpu.HBM)] * len(sources),
        out_specs=[WHOLE] * 7,
        scratch_shapes=[VMEM(a.shape, a.dtype) for a in sources]
        + [pltpu.SemaphoreType.DMA((len(sources),))],
        compiler_params=params(16),
        cost_estimate=cost(2 * window * capacity * tok_dev * width, 5 * tok_dev * width),
        name="prepare",
    )(*in_hbm(*sources))


def chosen(key_ref, refs):
    key = key_ref[:1, :1]
    value = refs[0][...].astype(F32)
    for i in range(1, len(refs)):
        value = jnp.where(key == i + 1, refs[i][...].astype(F32), value)
    return value.astype(BF16)


def pick_kernel(pair, key_ref, hit_ref, low_ref, *refs):
    count = hit_ref.shape[0] // pair
    shuffled = jnp.concatenate([low_ref[...], chosen(key_ref, refs[:-count])], axis=0)
    picked = jnp.dot(hit_ref[...], shuffled, preferred_element_type=F32).astype(BF16)
    for z, out in enumerate(refs[-count:]):
        out[...] = picked[z * pair : (z + 1) * pair]


def pick(key, hit, low, arrived, capacity):
    pair, width = 2 * capacity, low.shape[1]
    slots, tok_dev = hit.shape
    return pl.pallas_call(
        functools.partial(pick_kernel, pair),
        out_shape=[jax.ShapeDtypeStruct((pair, width), BF16)] * (slots // pair),
        in_specs=[WHOLE] * (3 + len(arrived)),
        out_specs=[WHOLE] * (slots // pair),
        compiler_params=params(12),
        cost_estimate=cost(2 * slots * tok_dev * width, 5 * tok_dev * width),
        name="pick",
    )(key, hit, low, *arrived)


def joined(direct, crossed, capacity):
    rows = lax.broadcasted_iota(jnp.int32, direct.shape, 0)
    return jnp.where(rows < capacity, direct[...].astype(F32), crossed[...].astype(F32)).astype(BF16)


def gather_kernel(weighted_ref, rows_ref, shares_ref):
    me = lax.axis_index("expert")
    window, capacity, _ = weighted_ref.shape
    pair = 2 * capacity
    for z in range(window // 2):
        both = [weighted_ref[me ^ (2 * z + core)].astype(F32) for core in range(2)]
        rows_ref[z * pair : (z + 1) * pair, :] = jnp.concatenate(both, axis=0).astype(BF16)
    share = shares_ref.shape[2]
    for g in range(shares_ref.shape[0]):
        shares_ref[g] = rows_ref[:, g * share : (g + 1) * share]


def gather_rows(weighted):
    window, capacity, width = weighted.shape
    rows = window * capacity
    replicas = lax.axis_size("dp")
    return pl.pallas_call(
        gather_kernel,
        out_shape=[
            jax.ShapeDtypeStruct((rows, width), BF16),
            jax.ShapeDtypeStruct((replicas, rows, width // replicas), BF16),
        ],
        in_specs=[WHOLE],
        out_specs=[WHOLE] * 2,
        compiler_params=params(12),
        cost_estimate=cost(0, 8 * rows * width),
        name="gather_rows",
    )(weighted)


def expert_kernel(sizes, *refs):
    count, capacity, tile, replicas = sizes
    x_refs, w_ref, weights = refs[: 2 * count], refs[2 * count], refs[2 * count + 1 : 2 * count + 4]
    tok_refs = refs[2 * count + 4 : 3 * count + 4]
    out_ref, sent_refs = refs[3 * count + 4], refs[3 * count + 5 : 3 * count + 5 + replicas]
    (x_all, hid_all, gg_all, gu_all, gate_ref, up_ref, down_ref, sems) = refs[
        3 * count + 5 + replicas :
    ]
    tiles = hid_all.shape[1] // tile
    copies = []
    for f in range(tiles):
        span = pl.ds(f * tile, tile)
        pieces = [
            (weights[0].at[0, :, span], gate_ref.at[0, :, span]),
            (weights[1].at[0, :, span], up_ref.at[0, :, span]),
            (weights[2].at[0, span, :], down_ref.at[0, span, :]),
        ]
        copies.append(
            [pltpu.make_async_copy(a, b, sems.at[f, i]) for i, (a, b) in enumerate(pieces)]
        )
    for group in copies:
        for copy in group:
            copy.start()
    me = lax.axis_index("expert")
    replica = lax.axis_index("dp")
    pair = 2 * capacity
    width = x_all.shape[1]
    share = width // replicas
    turned = (((1,), (1,)), ((), ()))
    for z in range(count):
        x_all[z * pair : (z + 1) * pair, :] = joined(x_refs[2 * z], x_refs[2 * z + 1], capacity)
    for j, sent in enumerate(sent_refs):
        columns = pl.ds(pl.multiple_of((replica ^ j) * share, share), share)
        sent[:, sent.shape[1] - share :] = x_all[:, columns]
    for f in range(tiles):
        span = slice(f * tile, (f + 1) * tile)
        for copy in copies[f]:
            copy.wait()
        pre_gate = jnp.dot(x_all[...], gate_ref[0, :, span], preferred_element_type=F32)
        pre_up = jnp.dot(x_all[...], up_ref[0, :, span], preferred_element_type=F32)
        grad_hidden = lax.dot_general(
            w_ref[...], down_ref[0, span, :], turned, preferred_element_type=F32
        )
        sig = jax.nn.sigmoid(pre_gate)
        silu = pre_gate * sig
        hid_all[:, span] = (silu * pre_up).astype(BF16)
        gg_all[:, span] = (
            grad_hidden * pre_up * sig * (1.0 + pre_gate * (1.0 - sig))
        ).astype(BF16)
        gu_all[:, span] = (grad_hidden * silu).astype(BF16)
        for sent in sent_refs:
            if sent.shape[1] > share:
                for k, source in enumerate((hid_all, gg_all, gu_all)):
                    sent[:, (3 * f + k) * tile : (3 * f + k + 1) * tile] = source[:, span]
    wide = 2 * tile
    for n in range(width // wide):
        span = slice(n * wide, (n + 1) * wide)
        tok = lax.dot_general(
            gg_all[...], gate_ref[0, span, :], turned, preferred_element_type=F32
        ) + lax.dot_general(gu_all[...], up_ref[0, span, :], turned, preferred_element_type=F32)
        tok = tok.astype(BF16)
        out = jnp.dot(hid_all[...], down_ref[0, :, span], preferred_element_type=F32)
        for z in range(count):
            tok_refs[z][:, span] = tok[z * pair : (z + 1) * pair]
        for d in range(2 * count):
            out_ref[me ^ d, :, span] = out[d * capacity : (d + 1) * capacity].astype(BF16)


def expert(x_pairs, w_rows, w_gate, w_up, w_down, capacity):
    count = len(x_pairs)
    flat = [a for p in x_pairs for a in p]
    pair, width = flat[0].shape
    hidden_units = w_gate.shape[2]
    rows = count * pair
    replicas = lax.axis_size("dp")
    share = width // replicas
    block = jax.ShapeDtypeStruct((pair, width), BF16)
    sent = [jax.ShapeDtypeStruct((rows, 3 * hidden_units + share), BF16)] * replicas
    if replicas == 4:
        sent[3] = jax.ShapeDtypeStruct((rows, share), BF16)
    results = pl.pallas_call(
        functools.partial(expert_kernel, (count, capacity, TILE, replicas)),
        out_shape=[block] * count
        + [jax.ShapeDtypeStruct((2 * count, capacity, width), BF16)]
        + sent,
        in_specs=[WHOLE] * (2 * count + 1) + [pl.BlockSpec(memory_space=pltpu.HBM)] * 3,
        out_specs=[WHOLE] * (count + 1 + replicas),
        scratch_shapes=[VMEM((rows, width), BF16)]
        + [VMEM((rows, hidden_units), BF16)] * 3
        + [VMEM(a.shape, BF16) for a in (w_gate, w_up, w_down)]
        + [pltpu.SemaphoreType.DMA((hidden_units // TILE, 3))],
        compiler_params=params(32 if replicas <= 4 else 56),
        cost_estimate=cost(
            12 * rows * width * hidden_units, 6 * width * hidden_units + 10 * rows * width
        ),
        name="expert",
    )(*flat, w_rows, *in_hbm(w_gate, w_up, w_down))
    return results[:count], results[count], results[count + 1 :]


def weight_kernel(sizes, w_ref, *refs):
    share, tile, parts = sizes
    sources, outs = refs[:-7], refs[-7:-4]
    held, sems = refs[-4:-1], refs[-1]
    me = lax.axis_index("dp")
    acts_width = sources[0].shape[1] - share
    across = (((0,), (0,)), ((), ()))
    x = jnp.concatenate([r[:, r.shape[1] - share :] for r in sources[:parts]], axis=0)
    w = jnp.concatenate([w_ref[me ^ j] for j in range(parts)], axis=0)
    acts = [r for r in sources if r.shape[1] > share]
    copies = []
    for f in range(acts_width // (3 * tile)):
        hidden, grad_gate, grad_up = [
            jnp.concatenate(
                [a[:, (3 * f + k) * tile : (3 * f + k + 1) * tile] for a in acts], axis=0
            )
            for k in range(3)
        ]
        span = pl.ds(f * tile, tile)
        gate_held, up_held, down_held = [h.at[f] for h in held]
        gate_held[...] = lax.dot_general(x, grad_gate, across, preferred_element_type=F32)
        up_held[...] = lax.dot_general(x, grad_up, across, preferred_element_type=F32)
        down_held[...] = lax.dot_general(hidden, w, across, preferred_element_type=F32)
        pieces = [
            (gate_held, outs[0].at[0, :, span]),
            (up_held, outs[1].at[0, :, span]),
            (down_held, outs[2].at[0, span, :]),
        ]
        for i, (a, b) in enumerate(pieces):
            copy = pltpu.make_async_copy(a, b, sems.at[f, i])
            copy.start()
            copies.append(copy)
    for copy in copies:
        copy.wait()


def weight_grads(w_shares, received):
    parts, rows, share = w_shares.shape
    hidden_units = (received[0].shape[1] - share) // 3
    tile = TILE
    tiles = hidden_units // tile
    return pl.pallas_call(
        functools.partial(weight_kernel, (share, tile, parts)),
        out_shape=[
            jax.ShapeDtypeStruct((1, share, hidden_units), F32),
            jax.ShapeDtypeStruct((1, share, hidden_units), F32),
            jax.ShapeDtypeStruct((1, hidden_units, share), F32),
        ],
        in_specs=[WHOLE] * (1 + len(received)),
        out_specs=[pl.BlockSpec(memory_space=pltpu.HBM)] * 3,
        scratch_shapes=[
            VMEM((tiles, share, tile), F32),
            VMEM((tiles, share, tile), F32),
            VMEM((tiles, tile, share), F32),
            pltpu.SemaphoreType.DMA((tiles, 3)),
        ],
        compiler_params=params(24 if parts <= 4 else 56),
        cost_estimate=cost(6 * parts * rows * share * hidden_units, 12 * share * hidden_units),
        name="weight_grads",
    )(w_shares, *received)


def output_kernel(high_ref, fine_ref, back_ref, out_ref):
    window, capacity, width = back_ref.shape
    rows = jnp.concatenate([back_ref[e].astype(F32) for e in range(window)], axis=0).astype(BF16)
    across = (((0,), (0,)), ((), ()))
    total = lax.dot_general(high_ref[...], rows, across, preferred_element_type=F32)
    total += lax.dot_general(fine_ref[...], rows, across, preferred_element_type=F32)
    out_ref[...] = total.astype(BF16)


def combine_output(high, fine, back):
    slots, tok_dev = high.shape
    width = back.shape[2]
    return pl.pallas_call(
        output_kernel,
        out_shape=jax.ShapeDtypeStruct((tok_dev, width), BF16),
        in_specs=[WHOLE] * 3,
        out_specs=WHOLE,
        compiler_params=params(12),
        cost_estimate=cost(4 * slots * tok_dev * width, 6 * tok_dev * width),
        name="combine_output",
    )(high, fine, back)


def grads_kernel(capacity, hit_ref, *refs):
    pairs, (low_ref, high_ref) = refs[:-2], refs[-2:]
    rows = jnp.concatenate(
        [joined(pairs[i], pairs[i + 1], capacity) for i in range(0, len(pairs), 2)], axis=0
    )
    across = (((0,), (0,)), ((), ()))
    total = lax.dot_general(hit_ref[...], rows, across, preferred_element_type=F32).astype(BF16)
    half = low_ref.shape[0]
    low_ref[...] = total[:half]
    high_ref[...] = total[half:]


def combine_grads(hit, pairs, capacity):
    slots, tok_dev = hit.shape
    flat = [a for p in pairs for a in p]
    width = flat[0].shape[1]
    half = jax.ShapeDtypeStruct((tok_dev // 2, width), BF16)
    return pl.pallas_call(
        functools.partial(grads_kernel, capacity),
        out_shape=[half, half],
        in_specs=[WHOLE] * (1 + len(flat)),
        out_specs=[WHOLE, WHOLE],
        compiler_params=params(12),
        cost_estimate=cost(2 * slots * tok_dev * width, 6 * tok_dev * width),
        name="combine_grads",
    )(hit, *flat)


def finish_kernel(key_ref, low_ref, *refs):
    out_ref = refs[-1]
    half = low_ref.shape[0]
    out_ref[:half] = low_ref[...]
    out_ref[half:] = chosen(key_ref, refs[:-1])


def finish(key, low, arrived):
    half, width = low.shape
    return pl.pallas_call(
        finish_kernel,
        out_shape=jax.ShapeDtypeStruct((2 * half, width), BF16),
        in_specs=[WHOLE] * (2 + len(arrived)),
        out_specs=WHOLE,
        compiler_params=params(12),
        cost_estimate=cost(0, 10 * half * width),
        name="finish",
    )(key, low, *arrived)


def exchange(blocks):
    direct = {0: blocks[0]}
    for z in range(len(blocks) - 1, 0, -1):
        direct[z] = xor_permute(blocks[z], "expert", 2 * z)
    return [(direct[z], xor_permute(direct[z], "expert", 1)) for z in range(len(blocks))]


def spread(array):
    return [array] + [xor_permute(array, "dp", j) for j in range(1, lax.axis_size("dp"))]


def spread_acts(sent):
    if lax.axis_size("dp") != 4:
        return [sent[0]] + [xor_permute(sent[j], "dp", j) for j in range(1, len(sent))]
    half = sent[0].shape[0] // 2
    acts = sent[0].shape[1] - sent[3].shape[1]
    near = xor_permute(sent[1], "dp", 1)
    side = xor_permute(sent[2], "dp", 2)
    far = xor_permute(sent[3], "dp", 3)
    halves = [
        xor_permute(side[:half, :acts], "dp", 1),
        xor_permute(near[half:, :acts], "dp", 2),
    ]
    return [sent[0], near, side, far, *halves]


def after(value, *others):
    return lax.optimization_barrier((value, *others))[0]


def all_to_all(array, axis):
    return lax.all_to_all(array, axis, split_axis=0, concat_axis=0, tiled=True)


def per_device(
    tokens,
    cotangent,
    w_gate,
    w_up,
    w_down,
    slot_rows,
    slot_counts,
    slot_gates,
    seq_lengths,
    matching,
):
    capacity = slot_rows.shape[2]
    moved, low, weighted, hit, high, fine, key = prepare(
        slot_rows, slot_gates, slot_counts, seq_lengths, matching, tokens, cotangent
    )
    weighted = all_to_all(weighted, "expert")
    w_rows, w_shares = gather_rows(weighted)
    picked = pick(key, hit, low, spread(moved)[1:], capacity)
    picked = [after(p, w_rows) for p in picked]
    x_pairs = exchange(picked)
    w_shares = all_to_all(w_shares, "dp")
    w_rows = after(w_rows, w_shares)
    token_rows, expert_out, sent = expert(x_pairs, w_rows, w_gate, w_up, w_down, capacity)
    tok_pairs = exchange(token_rows)
    received = spread_acts(sent)
    back = all_to_all(after(expert_out, *[p[0] for p in tok_pairs]), "expert")
    low_grads, high_grads = combine_grads(hit, tok_pairs, capacity)
    grad_tokens = finish(key, low_grads, spread(high_grads)[1:])
    grads = weight_grads(w_shares, received)
    output = combine_output(high, fine, back)
    return (output, grad_tokens, *grads)


def solution(mesh):
    return jax.shard_map(
        per_device,
        mesh=mesh,
        in_specs=(
            P(("dp", "expert"), None),
            P(("dp", "expert"), None),
            P("expert", None, None),
            P("expert", None, None),
            P("expert", None, None),
            P(("dp", "expert"), None, None),
            P(("dp", "expert"), None),
            P(("dp", "expert"), None, None),
            P(("dp", "expert"), None),
            P("expert", None),
        ),
        out_specs=(
            P(("dp", "expert"), None),
            P(("dp", "expert"), None),
            P("expert", "dp", None),
            P("expert", "dp", None),
            P("expert", None, "dp"),
        ),
        check_vma=False,
    )
```

```python
import functools

import jax
import jax.numpy as jnp
from jax import lax
from jax.experimental import pallas as pl
from jax.experimental.pallas import tpu as pltpu
from jax.sharding import PartitionSpec as P

F32 = jnp.float32
BF16 = jnp.bfloat16
VMEM = pltpu.VMEM
WHOLE = pl.BlockSpec(memory_space=pltpu.VMEM)
TILE = 256
PIECES = 4
MIB = 1024 * 1024


def params(mib):
    return pltpu.CompilerParams(vmem_limit_bytes=mib * MIB)


def in_hbm(*arrays):
    return [pltpu.with_memory_space_constraint(a, pltpu.HBM) for a in arrays]


def cost(flops, bytes_accessed):
    return pl.CostEstimate(flops=int(flops), bytes_accessed=int(bytes_accessed), transcendentals=0)


def xor_permute(array, axis, key):
    size = lax.axis_size(axis)
    return lax.ppermute(array, axis, [(i, i ^ key) for i in range(size)])


def column_of(row, length):
    diagonal = lax.broadcasted_iota(jnp.int32, (length, length), 0) == lax.broadcasted_iota(
        jnp.int32, (length, length), 1
    )
    spread = jnp.where(diagonal, jnp.broadcast_to(row.astype(F32), (length, length)), 0.0)
    return jnp.sum(spread, axis=1, keepdims=True)


def table_columns(table, order):
    return jnp.concatenate([column_of(row, row.shape[1]) for row in (table(e) for e in order)], axis=0)


def keep_valid(values, lengths, first_slot, slot_len):
    rows = lax.broadcasted_iota(jnp.int32, values.shape, 0)
    limit = jnp.zeros(values.shape, jnp.int32)
    for slot in range(values.shape[0] // slot_len):
        used = lengths[:, first_slot + slot : first_slot + slot + 1]
        limit = jnp.where(rows // slot_len == slot, slot * slot_len + used, limit)
    return jnp.where(rows < limit, values.astype(F32), 0.0).astype(values.dtype)


def prepare_kernel(sizes, *refs):
    window, capacity, tok_dev, slot_len = sizes
    sources, outs, held = refs[:6], refs[6:12], refs[12:18]
    high_held, fine_held, sems = refs[18:]
    copies = [
        pltpu.make_async_copy(source, place, sems.at[i])
        for i, (source, place) in enumerate(zip(sources, held))
    ]
    for copy in copies:
        copy.start()
    for copy in copies:
        copy.wait()
    rows_ref, gates_ref, counts_ref, lengths_ref, tok_ref, cot_ref = held
    moved_ref, low_ref, weighted_ref, hit_ref, high_ref, fine_ref = outs
    me = lax.axis_index("expert")
    half = tok_dev // 2
    lengths = lengths_ref[...]
    moved_ref[...] = keep_valid(tok_ref[half:, :], lengths, half // slot_len, slot_len)
    low_ref[...] = keep_valid(tok_ref[:half, :], lengths, 0, slot_len)

    def gate_of(e):
        slot = lax.broadcasted_iota(jnp.int32, (1, capacity), 1)
        owner = lax.broadcasted_iota(jnp.int32, (1, window), 1) == e
        count = jnp.sum(jnp.where(owner, counts_ref[...].astype(F32), 0.0), axis=1, keepdims=True)
        return jnp.where(slot.astype(F32) < count, gates_ref[0, pl.ds(e, 1), :], 0.0)

    order = [me ^ d for d in range(window)]
    gate = table_columns(gate_of, order)
    index = table_columns(lambda e: rows_ref[0, pl.ds(e, 1), :], order).astype(jnp.int32)
    hit = lax.broadcasted_iota(jnp.int32, (window * capacity, tok_dev), 1) == index
    hit_ref[...] = hit.astype(BF16)
    table = jnp.where(hit, jnp.broadcast_to(gate, hit.shape), 0.0)
    high = table.astype(BF16)
    high_held[...] = high
    fine_held[...] = (table - high.astype(F32)).astype(BF16)
    copies = [
        pltpu.make_async_copy(high_held, high_ref, sems.at[0]),
        pltpu.make_async_copy(fine_held, fine_ref, sems.at[1]),
    ]
    for copy in copies:
        copy.start()
    picked = jnp.dot(hit.astype(BF16), cot_ref[...], preferred_element_type=F32)
    weighted = gate * picked
    for d, e in enumerate(order):
        weighted_ref[e] = weighted[d * capacity : (d + 1) * capacity].astype(BF16)
    for copy in copies:
        copy.wait()


def prepare(slot_rows, slot_gates, slot_counts, seq_lengths, tokens, cotangent):
    tok_dev, width = tokens.shape
    window, capacity = slot_rows.shape[1:]
    half = tok_dev // 2
    slot_len = tok_dev // seq_lengths.shape[1]
    sources = (slot_rows, slot_gates, slot_counts, seq_lengths, tokens, cotangent)
    table = jax.ShapeDtypeStruct((window * capacity, tok_dev), BF16)
    return pl.pallas_call(
        functools.partial(prepare_kernel, (window, capacity, tok_dev, slot_len)),
        out_shape=[
            jax.ShapeDtypeStruct((half, width), BF16),
            jax.ShapeDtypeStruct((half, width), BF16),
            jax.ShapeDtypeStruct((window, capacity, width), BF16),
            table,
            pltpu.HBM(table.shape, table.dtype),
            pltpu.HBM(table.shape, table.dtype),
        ],
        in_specs=[pl.BlockSpec(memory_space=pltpu.HBM)] * len(sources),
        out_specs=[WHOLE] * 4 + [pl.BlockSpec(memory_space=pltpu.HBM)] * 2,
        scratch_shapes=[VMEM(a.shape, a.dtype) for a in sources]
        + [VMEM(table.shape, BF16)] * 2
        + [pltpu.SemaphoreType.DMA((len(sources),))],
        compiler_params=params(12),
        cost_estimate=cost(2 * window * capacity * tok_dev * width, 5 * tok_dev * width),
        name="prepare",
    )(*in_hbm(*sources))


def pick_kernel(pair, hit_ref, low_ref, arrived_ref, *outs):
    shuffled = jnp.concatenate([low_ref[...], arrived_ref[...]], axis=0)
    picked = jnp.dot(hit_ref[...], shuffled, preferred_element_type=F32).astype(BF16)
    for z, out in enumerate(outs):
        out[...] = picked[z * pair : (z + 1) * pair]


def pick(hit, low, arrived, capacity):
    pair, width = 2 * capacity, low.shape[1]
    slots, tok_dev = hit.shape
    return pl.pallas_call(
        functools.partial(pick_kernel, pair),
        out_shape=[jax.ShapeDtypeStruct((pair, width), BF16)] * (slots // pair),
        in_specs=[WHOLE] * 3,
        out_specs=[WHOLE] * (slots // pair),
        compiler_params=params(8),
        cost_estimate=cost(2 * slots * tok_dev * width, 5 * tok_dev * width),
        name="pick",
    )(hit, low, arrived)


def joined(direct, crossed, capacity, columns=slice(None)):
    one, other = direct[:, columns].astype(F32), crossed[:, columns].astype(F32)
    rows = lax.broadcasted_iota(jnp.int32, one.shape, 0)
    return jnp.where(rows < capacity, one, other).astype(BF16)


def share_columns(rows, outs):
    me = lax.axis_index("dp")
    share = outs[0].shape[1]
    for j, out in enumerate(outs):
        out[...] = rows[:, pl.ds(pl.multiple_of((me ^ j) * share, share), share)]


def gather_kernel(weighted_ref, rows_ref, shares_ref):
    me = lax.axis_index("expert")
    window, capacity, _ = weighted_ref.shape
    pair = 2 * capacity
    for z in range(window // 2):
        both = [weighted_ref[me ^ (2 * z + core)].astype(F32) for core in range(2)]
        rows_ref[z * pair : (z + 1) * pair, :] = jnp.concatenate(both, axis=0).astype(BF16)
    share = shares_ref.shape[2]
    for g in range(shares_ref.shape[0]):
        shares_ref[g] = rows_ref[:, g * share : (g + 1) * share]


def gather_rows(weighted):
    window, capacity, width = weighted.shape
    rows = window * capacity
    replicas = lax.axis_size("dp")
    return pl.pallas_call(
        gather_kernel,
        out_shape=[
            jax.ShapeDtypeStruct((rows, width), BF16),
            jax.ShapeDtypeStruct((replicas, rows, width // replicas), BF16),
        ],
        in_specs=[WHOLE],
        out_specs=[WHOLE] * 2,
        compiler_params=params(12),
        cost_estimate=cost(0, 8 * rows * width),
        name="gather_rows",
    )(weighted)


def expert_kernel(sizes, *refs):
    count, capacity, tile, replicas = sizes
    x_refs, w_ref, weights = refs[: 2 * count], refs[2 * count], refs[2 * count + 1 : 2 * count + 4]
    tok_refs = refs[2 * count + 4 : 3 * count + 4]
    out_ref, sent_refs = refs[3 * count + 4], refs[3 * count + 5 : 3 * count + 5 + replicas]
    x_all, hid_all, gg_all, gu_all, pre_gate, grad_hidden, own_held, *held, sems = refs[
        3 * count + 5 + replicas :
    ]
    own_copy = pltpu.make_async_copy(own_held, sent_refs[0], sems.at[3, 0])
    sent_refs = [own_held, *sent_refs[1:]]
    gate_ref, up_ref, down_ref = held
    copies = []
    for i, (source, place) in enumerate(zip(weights, held)):
        part = source.shape[1] // PIECES
        pieces = [pl.ds(k * part, part) for k in range(PIECES)]
        copies.append(
            [
                pltpu.make_async_copy(source.at[:, rows, :], place.at[:, rows, :], sems.at[i, k])
                for k, rows in enumerate(pieces)
            ]
        )
    for copy in copies[0] + copies[2]:
        copy.start()
    me = lax.axis_index("expert")
    pair = 2 * capacity
    width = x_all.shape[1]
    share = width // replicas
    turned = (((1,), (1,)), ((), ()))
    for z in range(count):
        x_all[z * pair : (z + 1) * pair, :] = joined(x_refs[2 * z], x_refs[2 * z + 1], capacity)
    share_columns(x_all, [s.at[:, s.shape[1] - share :] for s in sent_refs])
    spans = [slice(f * tile, (f + 1) * tile) for f in range(hid_all.shape[1] // tile)]
    for copy in copies[0]:
        copy.wait()
    for copy in copies[1]:
        copy.start()
    for span in spans:
        pre_gate[:, span] = jnp.dot(x_all[...], gate_ref[0, :, span], preferred_element_type=F32)
    for copy in copies[2]:
        copy.wait()
    for span in spans:
        grad_hidden[:, span] = lax.dot_general(
            w_ref[...], down_ref[0, span, :], turned, preferred_element_type=F32
        )
    for copy in copies[1]:
        copy.wait()
    for f, span in enumerate(spans):
        gate, grad = pre_gate[:, span], grad_hidden[:, span]
        pre_up = jnp.dot(x_all[...], up_ref[0, :, span], preferred_element_type=F32)
        sig = jax.nn.sigmoid(gate)
        silu = gate * sig
        hid_all[:, span] = (silu * pre_up).astype(BF16)
        gg_all[:, span] = (grad * pre_up * sig * (1.0 + gate * (1.0 - sig))).astype(BF16)
        gu_all[:, span] = (grad * silu).astype(BF16)
        for sent in sent_refs:
            if sent.shape[1] > share:
                for k, source in enumerate((hid_all, gg_all, gu_all)):
                    sent[:, (3 * f + k) * tile : (3 * f + k + 1) * tile] = source[:, span]
    own_copy.start()
    wide = 2 * tile
    for n in range(width // wide):
        span = slice(n * wide, (n + 1) * wide)
        tok = lax.dot_general(
            gg_all[...], gate_ref[0, span, :], turned, preferred_element_type=F32
        ) + lax.dot_general(gu_all[...], up_ref[0, span, :], turned, preferred_element_type=F32)
        tok = tok.astype(BF16)
        out = jnp.dot(hid_all[...], down_ref[0, :, span], preferred_element_type=F32)
        for z in range(count):
            tok_refs[z][:, span] = tok[z * pair : (z + 1) * pair]
        for d in range(2 * count):
            out_ref[me ^ d, :, span] = out[d * capacity : (d + 1) * capacity].astype(BF16)
    own_copy.wait()


def expert(x_pairs, w_rows, w_gate, w_up, w_down, capacity):
    count = len(x_pairs)
    flat = [a for p in x_pairs for a in p]
    pair, width = flat[0].shape
    hidden_units = w_gate.shape[2]
    rows = count * pair
    replicas = lax.axis_size("dp")
    share = width // replicas
    block = jax.ShapeDtypeStruct((pair, width), BF16)
    sent = [jax.ShapeDtypeStruct((rows, 3 * hidden_units + share), BF16)] * replicas
    if replicas == 4:
        sent[3] = jax.ShapeDtypeStruct((rows, share), BF16)
    sent[0] = pltpu.HBM(sent[0].shape, sent[0].dtype)
    results = pl.pallas_call(
        functools.partial(expert_kernel, (count, capacity, TILE, replicas)),
        out_shape=[block] * count
        + [jax.ShapeDtypeStruct((2 * count, capacity, width), BF16)]
        + sent,
        in_specs=[WHOLE] * (2 * count + 1) + [pl.BlockSpec(memory_space=pltpu.HBM)] * 3,
        out_specs=[WHOLE] * (count + 1)
        + [pl.BlockSpec(memory_space=pltpu.HBM)]
        + [WHOLE] * (replicas - 1),
        scratch_shapes=[VMEM((rows, width), BF16)]
        + [VMEM((rows, hidden_units), BF16)] * 3
        + [VMEM((rows, hidden_units), F32)] * 2
        + [VMEM(sent[0].shape, BF16)]
        + [VMEM(a.shape, BF16) for a in (w_gate, w_up, w_down)]
        + [pltpu.SemaphoreType.DMA((4, PIECES))],
        compiler_params=params(32 if replicas <= 4 else 56),
        cost_estimate=cost(
            12 * rows * width * hidden_units, 6 * width * hidden_units + 10 * rows * width
        ),
        name="expert",
    )(*flat, w_rows, *in_hbm(w_gate, w_up, w_down))
    return results[:count], results[count], results[count + 1 :]


def final_kernel(sizes, *refs):
    share, tile, parts = sizes
    loads, refs = list(refs[:3]), refs[3:]
    low_ref, arrived_ref, back_ref, w_ref, refs = *refs[:4], refs[4:]
    others, outs, scratch = refs[:-14], refs[-14:-9], refs[-9:]
    own_held, high_ref, fine_ref, out_held, *held, sems, side_sems = scratch
    loads = [
        pltpu.make_async_copy(a, b, side_sems.at[i])
        for i, (a, b) in enumerate(zip(loads, (own_held, high_ref, fine_ref)))
    ]
    half = low_ref.shape[0]
    stores = [
        pltpu.make_async_copy(low_ref, outs[1].at[:half], side_sems.at[3]),
        pltpu.make_async_copy(arrived_ref, outs[1].at[half:], side_sems.at[4]),
    ]
    for copy in loads + stores:
        copy.start()
    for copy in loads:
        copy.wait()
    me = lax.axis_index("dp")
    sources = [own_held, *others]
    acts_width = sources[0].shape[1] - share
    across = (((0,), (0,)), ((), ()))
    x = jnp.concatenate([r[:, r.shape[1] - share :] for r in sources[:parts]], axis=0)
    w = jnp.concatenate([w_ref[me ^ j] for j in range(parts)], axis=0)
    acts = [r for r in sources if r.shape[1] > share]
    for f in range(acts_width // (3 * tile)):
        hidden, grad_gate, grad_up = [
            jnp.concatenate(
                [a[:, (3 * f + k) * tile : (3 * f + k + 1) * tile] for a in acts], axis=0
            )
            for k in range(3)
        ]
        span = pl.ds(f * tile, tile)
        gate_held, up_held, down_held = [h.at[f] for h in held]
        gate_held[...] = lax.dot_general(x, grad_gate, across, preferred_element_type=F32)
        up_held[...] = lax.dot_general(x, grad_up, across, preferred_element_type=F32)
        down_held[...] = lax.dot_general(hidden, w, across, preferred_element_type=F32)
        pieces = [
            (gate_held, outs[2].at[0, :, span]),
            (up_held, outs[3].at[0, :, span]),
            (down_held, outs[4].at[0, span, :]),
        ]
        for i, (a, b) in enumerate(pieces):
            copy = pltpu.make_async_copy(a, b, sems.at[f, i])
            copy.start()
            stores.append(copy)
    expert_id = lax.axis_index("expert")
    rows = jnp.concatenate(
        [back_ref[expert_id ^ d].astype(F32) for d in range(back_ref.shape[0])], axis=0
    ).astype(BF16)
    total = lax.dot_general(high_ref[...], rows, across, preferred_element_type=F32)
    total += lax.dot_general(fine_ref[...], rows, across, preferred_element_type=F32)
    out_held[...] = total.astype(BF16)
    stores.append(pltpu.make_async_copy(out_held, outs[0], side_sems.at[5]))
    stores[-1].start()
    for copy in stores:
        copy.wait()


def final(high, fine, back, low, arrived, w_shares, received):
    parts, rows, share = w_shares.shape
    half, width = low.shape
    hidden_units = (received[0].shape[1] - share) // 3
    tile = TILE
    tiles = hidden_units // tile
    hbm = pl.BlockSpec(memory_space=pltpu.HBM)
    return pl.pallas_call(
        functools.partial(final_kernel, (share, tile, parts)),
        out_shape=[
            jax.ShapeDtypeStruct((2 * half, width), BF16),
            jax.ShapeDtypeStruct((2 * half, width), BF16),
            jax.ShapeDtypeStruct((1, share, hidden_units), F32),
            jax.ShapeDtypeStruct((1, share, hidden_units), F32),
            jax.ShapeDtypeStruct((1, hidden_units, share), F32),
        ],
        in_specs=[hbm] * 3 + [WHOLE] * (3 + len(received)),
        out_specs=[hbm] * 5,
        scratch_shapes=[
            VMEM(received[0].shape, BF16),
            VMEM(high.shape, BF16),
            VMEM(fine.shape, BF16),
            VMEM((2 * half, width), BF16),
            VMEM((tiles, share, tile), F32),
            VMEM((tiles, share, tile), F32),
            VMEM((tiles, tile, share), F32),
            pltpu.SemaphoreType.DMA((tiles, 3)),
            pltpu.SemaphoreType.DMA((6,)),
        ],
        compiler_params=params(24 if parts <= 4 else 60),
        cost_estimate=cost(6 * parts * rows * share * hidden_units, 12 * share * hidden_units),
        name="final",
    )(*in_hbm(received[0], high, fine), low, arrived, back, w_shares, *received[1:])


def grads_kernel(capacity, hit_ref, *refs):
    pairs, (low_ref, high_ref) = refs[:-2], refs[-2:]
    rows = jnp.concatenate(
        [joined(pairs[i], pairs[i + 1], capacity) for i in range(0, len(pairs), 2)], axis=0
    )
    across = (((0,), (0,)), ((), ()))
    total = lax.dot_general(hit_ref[...], rows, across, preferred_element_type=F32).astype(BF16)
    half = low_ref.shape[0]
    low_ref[...] = total[:half]
    high_ref[...] = total[half:]


def combine_grads(hit, pairs, capacity):
    slots, tok_dev = hit.shape
    flat = [a for p in pairs for a in p]
    width = flat[0].shape[1]
    half = jax.ShapeDtypeStruct((tok_dev // 2, width), BF16)
    return pl.pallas_call(
        functools.partial(grads_kernel, capacity),
        out_shape=[half, half],
        in_specs=[WHOLE] * (1 + len(flat)),
        out_specs=[WHOLE, WHOLE],
        compiler_params=params(12),
        cost_estimate=cost(2 * slots * tok_dev * width, 6 * tok_dev * width),
        name="combine_grads",
    )(hit, *flat)


def send_chips(blocks):
    return [xor_permute(b, "expert", 2 * z) if z else b for z, b in enumerate(blocks)]


def cross(direct, waits=()):
    return [
        (block, xor_permute(after(block, *waits) if z else block, "expert", 1))
        for z, block in enumerate(direct)
    ]


def swapped(array, key):
    ways = [
        functools.partial(xor_permute, axis="dp", key=j) for j in range(1, lax.axis_size("dp"))
    ]
    return lax.switch(key - 1, ways, array)


def spread_acts(sent):
    if lax.axis_size("dp") != 4:
        return [sent[0]] + [xor_permute(sent[j], "dp", j) for j in range(1, len(sent))], []
    half = sent[0].shape[0] // 2
    near = xor_permute(sent[1], "dp", 1)
    side = xor_permute(sent[2], "dp", 2)
    far = xor_permute(sent[3], "dp", 3)
    passed = [side[:half], near[half:]]
    halves = [xor_permute(passed[0], "dp", 1), xor_permute(passed[1], "dp", 2)]
    return [sent[0], near, side, far, *halves], passed


def after(value, *others):
    return lax.optimization_barrier((value, *others))[0] if others else value


def all_to_all(array, axis):
    return lax.all_to_all(array, axis, split_axis=0, concat_axis=0, tiled=True)


def per_device(
    tokens,
    cotangent,
    w_gate,
    w_up,
    w_down,
    slot_rows,
    slot_counts,
    slot_gates,
    seq_lengths,
    matching,
):
    capacity = slot_rows.shape[2]
    key = matching[0, 0]
    moved, low, weighted, hit, high, fine = prepare(
        slot_rows, slot_gates, slot_counts, seq_lengths, tokens, cotangent
    )
    weighted = all_to_all(weighted, "expert")
    picked = pick(hit, low, swapped(moved, key), capacity)
    x_direct = send_chips(picked)
    w_rows, w_shares = gather_rows(weighted)
    w_shares = all_to_all(w_shares, "dp")
    x_pairs = cross(x_direct, [w_rows])
    token_rows, expert_out, sent = expert(x_pairs, w_rows, w_gate, w_up, w_down, capacity)
    tok_pairs = cross(send_chips(token_rows))
    received, early = spread_acts(sent)
    back = all_to_all(after(expert_out, w_shares, *[p[0] for p in tok_pairs]), "expert")
    low_grads, high_grads = combine_grads(hit, tok_pairs, capacity)
    return tuple(
        final(high, fine, back, low_grads, swapped(high_grads, key), w_shares, received)
    )


def solution(mesh):
    return jax.shard_map(
        per_device,
        mesh=mesh,
        in_specs=(
            P(("dp", "expert"), None),
            P(("dp", "expert"), None),
            P("expert", None, None),
            P("expert", None, None),
            P("expert", None, None),
            P(("dp", "expert"), None, None),
            P(("dp", "expert"), None),
            P(("dp", "expert"), None, None),
            P(("dp", "expert"), None),
            P("expert", None),
        ),
        out_specs=(
            P(("dp", "expert"), None),
            P(("dp", "expert"), None),
            P("expert", "dp", None),
            P("expert", "dp", None),
            P("expert", None, "dp"),
        ),
        check_vma=False,
    )
```

```python
import functools

import jax
import jax.numpy as jnp
from jax import lax
from jax.experimental import pallas as pl
from jax.experimental.pallas import tpu as pltpu
from jax.sharding import PartitionSpec as P

F32 = jnp.float32
BF16 = jnp.bfloat16
VMEM = pltpu.VMEM
WHOLE = pl.BlockSpec(memory_space=pltpu.VMEM)
TILE = 256
PIECES = 4
MIB = 1024 * 1024


def params(mib):
    return pltpu.CompilerParams(vmem_limit_bytes=mib * MIB)


def in_hbm(*arrays):
    return [pltpu.with_memory_space_constraint(a, pltpu.HBM) for a in arrays]


def cost(flops, bytes_accessed):
    return pl.CostEstimate(flops=int(flops), bytes_accessed=int(bytes_accessed), transcendentals=0)


def xor_permute(array, axis, key):
    size = lax.axis_size(axis)
    return lax.ppermute(array, axis, [(i, i ^ key) for i in range(size)])


def column_of(row, length):
    diagonal = lax.broadcasted_iota(jnp.int32, (length, length), 0) == lax.broadcasted_iota(
        jnp.int32, (length, length), 1
    )
    spread = jnp.where(diagonal, jnp.broadcast_to(row.astype(F32), (length, length)), 0.0)
    return jnp.sum(spread, axis=1, keepdims=True)


def table_columns(table, order):
    return jnp.concatenate([column_of(row, row.shape[1]) for row in (table(e) for e in order)], axis=0)


def keep_valid(values, lengths, first_slot, slot_len):
    rows = lax.broadcasted_iota(jnp.int32, values.shape, 0)
    limit = jnp.zeros(values.shape, jnp.int32)
    for slot in range(values.shape[0] // slot_len):
        used = lengths[:, first_slot + slot : first_slot + slot + 1]
        limit = jnp.where(rows // slot_len == slot, slot * slot_len + used, limit)
    return jnp.where(rows < limit, values.astype(F32), 0.0).astype(values.dtype)


def prepare_kernel(sizes, *refs):
    window, capacity, tok_dev, slot_len = sizes
    sources, outs, held = refs[:6], refs[6:12], refs[12:18]
    high_held, fine_held, weighted_held, sems, out_sems = refs[18:]
    copies = [
        pltpu.make_async_copy(source, place, sems.at[i])
        for i, (source, place) in enumerate(zip(sources, held))
    ]
    for i in (0, 1, 2, 5, 3, 4):
        copies[i].start()
    rows_ref, gates_ref, counts_ref, lengths_ref, tok_ref, cot_ref = held
    moved_ref, low_ref, weighted_ref, hit_ref, high_ref, fine_ref = outs
    me = lax.axis_index("expert")
    half = tok_dev // 2
    pair = 2 * capacity
    for i in (0, 1, 2, 5):
        copies[i].wait()

    def gate_of(e):
        slot = lax.broadcasted_iota(jnp.int32, (1, capacity), 1)
        owner = lax.broadcasted_iota(jnp.int32, (1, window), 1) == e
        count = jnp.sum(jnp.where(owner, counts_ref[...].astype(F32), 0.0), axis=1, keepdims=True)
        return jnp.where(slot.astype(F32) < count, gates_ref[0, pl.ds(e, 1), :], 0.0)

    order = [me ^ d for d in range(window)]
    gate = table_columns(gate_of, order)
    index = table_columns(lambda e: rows_ref[0, pl.ds(e, 1), :], order).astype(jnp.int32)
    hit = lax.broadcasted_iota(jnp.int32, (window * capacity, tok_dev), 1) == index
    picked = jnp.dot(hit.astype(BF16), cot_ref[...], preferred_element_type=F32)
    weighted = gate * picked
    swapped_cores = me % 2 == 1
    for z in range(window // 2):
        one = weighted[z * pair : z * pair + capacity]
        other = weighted[z * pair + capacity : (z + 1) * pair]
        block = jnp.where(
            swapped_cores,
            jnp.concatenate([other, one], axis=0),
            jnp.concatenate([one, other], axis=0),
        )
        weighted_held[(me // 2) ^ z] = block.astype(BF16)
    hit_ref[...] = hit.astype(BF16)
    table = jnp.where(hit, jnp.broadcast_to(gate, hit.shape), 0.0)
    high = table.astype(BF16)
    high_held[...] = high
    fine_held[...] = (table - high.astype(F32)).astype(BF16)
    stores = [
        pltpu.make_async_copy(a, b, out_sems.at[i])
        for i, (a, b) in enumerate(
            ((weighted_held, weighted_ref), (high_held, high_ref), (fine_held, fine_ref))
        )
    ]
    for copy in stores:
        copy.start()
    for i in (3, 4):
        copies[i].wait()
    lengths = lengths_ref[...]
    moved_ref[...] = keep_valid(tok_ref[half:, :], lengths, half // slot_len, slot_len)
    low_ref[...] = keep_valid(tok_ref[:half, :], lengths, 0, slot_len)
    for copy in stores:
        copy.wait()


def prepare(slot_rows, slot_gates, slot_counts, seq_lengths, tokens, cotangent):
    tok_dev, width = tokens.shape
    window, capacity = slot_rows.shape[1:]
    half = tok_dev // 2
    slot_len = tok_dev // seq_lengths.shape[1]
    sources = (slot_rows, slot_gates, slot_counts, seq_lengths, tokens, cotangent)
    table = jax.ShapeDtypeStruct((window * capacity, tok_dev), BF16)
    return pl.pallas_call(
        functools.partial(prepare_kernel, (window, capacity, tok_dev, slot_len)),
        out_shape=[
            jax.ShapeDtypeStruct((half, width), BF16),
            jax.ShapeDtypeStruct((half, width), BF16),
            pltpu.HBM((window // 2, 2 * capacity, width), BF16),
            table,
            pltpu.HBM(table.shape, table.dtype),
            pltpu.HBM(table.shape, table.dtype),
        ],
        in_specs=[pl.BlockSpec(memory_space=pltpu.HBM)] * len(sources),
        out_specs=[WHOLE] * 2
        + [pl.BlockSpec(memory_space=pltpu.HBM), WHOLE]
        + [pl.BlockSpec(memory_space=pltpu.HBM)] * 2,
        scratch_shapes=[VMEM(a.shape, a.dtype) for a in sources]
        + [VMEM(table.shape, BF16)] * 2
        + [VMEM((window // 2, 2 * capacity, width), BF16)]
        + [pltpu.SemaphoreType.DMA((len(sources),)), pltpu.SemaphoreType.DMA((3,))],
        compiler_params=params(12),
        cost_estimate=cost(2 * window * capacity * tok_dev * width, 5 * tok_dev * width),
        name="prepare",
    )(*in_hbm(*sources))


def pick_kernel(pair, hit_ref, low_ref, arrived_ref, *outs):
    shuffled = jnp.concatenate([low_ref[...], arrived_ref[...]], axis=0)
    picked = jnp.dot(hit_ref[...], shuffled, preferred_element_type=F32).astype(BF16)
    for z, out in enumerate(outs):
        out[...] = picked[z * pair : (z + 1) * pair]


def pick(hit, low, arrived, capacity):
    pair, width = 2 * capacity, low.shape[1]
    slots, tok_dev = hit.shape
    return pl.pallas_call(
        functools.partial(pick_kernel, pair),
        out_shape=[jax.ShapeDtypeStruct((pair, width), BF16)] * (slots // pair),
        in_specs=[WHOLE] * 3,
        out_specs=[WHOLE] * (slots // pair),
        compiler_params=params(8),
        cost_estimate=cost(2 * slots * tok_dev * width, 5 * tok_dev * width),
        name="pick",
    )(hit, low, arrived)


def joined(direct, crossed, capacity, columns=slice(None)):
    one, other = direct[:, columns].astype(F32), crossed[:, columns].astype(F32)
    rows = lax.broadcasted_iota(jnp.int32, one.shape, 0)
    return jnp.where(rows < capacity, one, other).astype(BF16)


def share_columns(rows, outs):
    me = lax.axis_index("dp")
    share = outs[1].shape[1]
    for j, out in enumerate(outs):
        if out is None:
            continue
        out[...] = rows[:, pl.ds(pl.multiple_of((me ^ j) * share, share), share)]


def gather_kernel(weighted_ref, rows_ref, shares_ref):
    me = lax.axis_index("expert")
    window, capacity, _ = weighted_ref.shape
    pair = 2 * capacity
    for z in range(window // 2):
        both = [weighted_ref[me ^ (2 * z + core)].astype(F32) for core in range(2)]
        rows_ref[z * pair : (z + 1) * pair, :] = jnp.concatenate(both, axis=0).astype(BF16)
    share = shares_ref.shape[2]
    for g in range(shares_ref.shape[0]):
        shares_ref[g] = rows_ref[:, g * share : (g + 1) * share]


def gather_rows(weighted):
    window, capacity, width = weighted.shape
    rows = window * capacity
    replicas = lax.axis_size("dp")
    return pl.pallas_call(
        gather_kernel,
        out_shape=[
            jax.ShapeDtypeStruct((rows, width), BF16),
            jax.ShapeDtypeStruct((replicas, rows, width // replicas), BF16),
        ],
        in_specs=[WHOLE],
        out_specs=[WHOLE] * 2,
        compiler_params=params(12),
        cost_estimate=cost(0, 8 * rows * width),
        name="gather_rows",
    )(weighted)


def expert_kernel(sizes, *refs):
    count, capacity, tile, replicas = sizes
    x_refs, w_ref, weights = refs[: 2 * count], refs[2 * count], refs[2 * count + 1 : 2 * count + 4]
    tok_refs = refs[2 * count + 4 : 3 * count + 4]
    out_ref, sent_refs = refs[3 * count + 4], refs[3 * count + 5 : 3 * count + 5 + replicas]
    x_all, hid_all, gg_all, gu_all, pre_gate, grad_hidden, *held, sems = refs[
        3 * count + 5 + replicas :
    ]
    wide_count = sum(ref.shape[1] > sent_refs[0].shape[1] for ref in sent_refs)
    sent_held, held = held[3:], held[:3]
    sent_copies = [
        pltpu.make_async_copy(a, b, sems.at[3, 1 + i])
        for i, (a, b) in enumerate(zip(sent_held, sent_refs[1 : 1 + wide_count]))
    ]
    sent_refs = [sent_refs[0], *sent_held, *sent_refs[1 + wide_count :]]
    gate_ref, up_ref, down_ref = held
    copies = []
    for i, (source, place) in enumerate(zip(weights, held)):
        part = source.shape[1] // PIECES
        pieces = [pl.ds(k * part, part) for k in range(PIECES)]
        copies.append(
            [
                pltpu.make_async_copy(source.at[:, rows, :], place.at[:, rows, :], sems.at[i, k])
                for k, rows in enumerate(pieces)
            ]
        )
    for copy in copies[0] + copies[2]:
        copy.start()
    me = lax.axis_index("expert")
    pair = 2 * capacity
    width = x_all.shape[1]
    share = width // replicas
    turned = (((1,), (1,)), ((), ()))
    for z in range(count):
        x_all[z * pair : (z + 1) * pair, :] = joined(x_refs[2 * z], x_refs[2 * z + 1], capacity)
    own = pl.ds(pl.multiple_of(lax.axis_index("dp") * share, share), share)
    own_copy = pltpu.make_async_copy(x_all.at[:, own], sent_refs[0], sems.at[3, 0])
    own_copy.start()
    share_columns(x_all, [None] + [s.at[:, s.shape[1] - share :] for s in sent_refs[1:]])
    spans = [slice(f * tile, (f + 1) * tile) for f in range(hid_all.shape[1] // tile)]
    for copy in copies[0]:
        copy.wait()
    for copy in copies[1]:
        copy.start()
    for span in spans:
        pre_gate[:, span] = jnp.dot(x_all[...], gate_ref[0, :, span], preferred_element_type=F32)
    for copy in copies[2]:
        copy.wait()
    for span in spans:
        grad_hidden[:, span] = lax.dot_general(
            w_ref[...], down_ref[0, span, :], turned, preferred_element_type=F32
        )
    for copy in copies[1]:
        copy.wait()
    for f, span in enumerate(spans):
        gate, grad = pre_gate[:, span], grad_hidden[:, span]
        pre_up = jnp.dot(x_all[...], up_ref[0, :, span], preferred_element_type=F32)
        sig = jax.nn.sigmoid(gate)
        silu = gate * sig
        hid_all[:, span] = (silu * pre_up).astype(BF16)
        gg_all[:, span] = (grad * pre_up * sig * (1.0 + gate * (1.0 - sig))).astype(BF16)
        gu_all[:, span] = (grad * silu).astype(BF16)
        for sent in sent_refs[1:]:
            if sent.shape[1] > share:
                for k, source in enumerate((hid_all, gg_all, gu_all)):
                    sent[:, (3 * f + k) * tile : (3 * f + k + 1) * tile] = source[:, span]
    for copy in sent_copies:
        copy.start()
    wide = 2 * tile
    for n in range(width // wide):
        span = slice(n * wide, (n + 1) * wide)
        tok = lax.dot_general(
            gg_all[...], gate_ref[0, span, :], turned, preferred_element_type=F32
        ) + lax.dot_general(gu_all[...], up_ref[0, span, :], turned, preferred_element_type=F32)
        tok = tok.astype(BF16)
        out = jnp.dot(hid_all[...], down_ref[0, :, span], preferred_element_type=F32)
        swapped_cores = me % 2 == 1
        for z in range(count):
            tok_refs[z][:, span] = tok[z * pair : (z + 1) * pair]
        for z in range(count):
            one = out[z * pair : z * pair + capacity]
            other = out[z * pair + capacity : (z + 1) * pair]
            block = jnp.where(
                swapped_cores,
                jnp.concatenate([other, one], axis=0),
                jnp.concatenate([one, other], axis=0),
            )
            out_ref[(me // 2) ^ z, :, span] = block.astype(BF16)
    for copy in [own_copy, *sent_copies]:
        copy.wait()


def expert(x_pairs, w_rows, w_gate, w_up, w_down, capacity):
    count = len(x_pairs)
    flat = [a for p in x_pairs for a in p]
    pair, width = flat[0].shape
    hidden_units = w_gate.shape[2]
    rows = count * pair
    replicas = lax.axis_size("dp")
    share = width // replicas
    block = jax.ShapeDtypeStruct((pair, width), BF16)
    sent = [jax.ShapeDtypeStruct((rows, 3 * hidden_units + share), BF16)] * replicas
    if replicas == 4:
        sent[3] = jax.ShapeDtypeStruct((rows, share), BF16)
    sent[0] = pltpu.HBM((rows, share), BF16)
    large = [a for a in sent[1:] if a.shape[1] > share]
    sent[1 : 1 + len(large)] = [pltpu.HBM(a.shape, BF16) for a in large]
    results = pl.pallas_call(
        functools.partial(expert_kernel, (count, capacity, TILE, replicas)),
        out_shape=[block] * count
        + [jax.ShapeDtypeStruct((count, pair, width), BF16)]
        + sent,
        in_specs=[WHOLE] * (2 * count + 1) + [pl.BlockSpec(memory_space=pltpu.HBM)] * 3,
        out_specs=[WHOLE] * (count + 1)
        + [pl.BlockSpec(memory_space=pltpu.HBM)] * (1 + len(large))
        + [WHOLE] * (replicas - 1 - len(large)),
        scratch_shapes=[VMEM((rows, width), BF16)]
        + [VMEM((rows, hidden_units), BF16)] * 3
        + [VMEM((rows, hidden_units), F32)] * 2
        + [VMEM(a.shape, BF16) for a in (w_gate, w_up, w_down, *large)]
        + [pltpu.SemaphoreType.DMA((4, max(PIECES, 1 + len(large))))],
        compiler_params=params(32 if replicas <= 4 else 56),
        cost_estimate=cost(
            12 * rows * width * hidden_units, 6 * width * hidden_units + 10 * rows * width
        ),
        name="expert",
    )(*flat, w_rows, *in_hbm(w_gate, w_up, w_down))
    return (
        results[:count],
        results[count].reshape(2 * count, capacity, width),
        results[count + 1 :],
    )


def final_kernel(sizes, *refs):
    share, tile, parts = sizes
    loads, refs = list(refs[:4]), refs[4:]
    back_ref, low_ref, arrived_ref, w_ref, refs = *refs[:4], refs[4:]
    sources, outs, scratch = refs[:-15], refs[-15:-10], refs[-10:]
    own_share, own_acts, high_ref, fine_ref, out_held, *held, sems, side_sems = scratch
    loads = [
        pltpu.make_async_copy(a, b, side_sems.at[i])
        for i, (a, b) in enumerate(zip(loads, (own_share, own_acts, high_ref, fine_ref)))
    ]
    half = low_ref.shape[0]
    stores = [
        pltpu.make_async_copy(low_ref, outs[1].at[:half], side_sems.at[4]),
        pltpu.make_async_copy(arrived_ref, outs[1].at[half:], side_sems.at[5]),
    ]
    for copy in loads + stores:
        copy.start()
    for copy in loads[:2]:
        copy.wait()
    sources = [own_share, *sources]
    me = lax.axis_index("dp")
    acts_width = own_acts.shape[1] - share
    across = (((0,), (0,)), ((), ()))
    x = jnp.concatenate([r[:, r.shape[1] - share :] for r in sources[:parts]], axis=0)
    w = jnp.concatenate([w_ref[me ^ j] for j in range(parts)], axis=0)
    acts = [own_acts] + [r for r in sources if r.shape[1] > share]
    for f in range(acts_width // (3 * tile)):
        hidden, grad_gate, grad_up = [
            jnp.concatenate(
                [a[:, (3 * f + k) * tile : (3 * f + k + 1) * tile] for a in acts], axis=0
            )
            for k in range(3)
        ]
        span = pl.ds(f * tile, tile)
        gate_held, up_held, down_held = [h.at[f] for h in held]
        gate_held[...] = lax.dot_general(x, grad_gate, across, preferred_element_type=F32)
        up_held[...] = lax.dot_general(x, grad_up, across, preferred_element_type=F32)
        down_held[...] = lax.dot_general(hidden, w, across, preferred_element_type=F32)
        pieces = [
            (gate_held, outs[2].at[0, :, span]),
            (up_held, outs[3].at[0, :, span]),
            (down_held, outs[4].at[0, span, :]),
        ]
        for i, (a, b) in enumerate(pieces):
            copy = pltpu.make_async_copy(a, b, sems.at[f, i])
            copy.start()
            stores.append(copy)
    for copy in loads[2:]:
        copy.wait()
    expert_id = lax.axis_index("expert")
    rows = jnp.concatenate(
        [back_ref[expert_id ^ d].astype(F32) for d in range(back_ref.shape[0])], axis=0
    ).astype(BF16)
    total = lax.dot_general(high_ref[...], rows, across, preferred_element_type=F32)
    total += lax.dot_general(fine_ref[...], rows, across, preferred_element_type=F32)
    out_held[...] = total.astype(BF16)
    stores.append(pltpu.make_async_copy(out_held, outs[0], side_sems.at[6]))
    stores[-1].start()
    for copy in stores:
        copy.wait()


def final(high, fine, back, low, arrived, w_shares, own_acts, received):
    parts, rows, share = w_shares.shape
    half, width = low.shape
    hidden_units = (own_acts.shape[1] - share) // 3
    tile = TILE
    tiles = hidden_units // tile
    hbm = pl.BlockSpec(memory_space=pltpu.HBM)
    return pl.pallas_call(
        functools.partial(final_kernel, (share, tile, parts)),
        out_shape=[
            jax.ShapeDtypeStruct((2 * half, width), BF16),
            jax.ShapeDtypeStruct((2 * half, width), BF16),
            jax.ShapeDtypeStruct((1, share, hidden_units), F32),
            jax.ShapeDtypeStruct((1, share, hidden_units), F32),
            jax.ShapeDtypeStruct((1, hidden_units, share), F32),
        ],
        in_specs=[hbm] * 4 + [WHOLE] * (3 + len(received)),
        out_specs=[hbm] * 5,
        scratch_shapes=[
            VMEM(received[0].shape, BF16),
            VMEM(own_acts.shape, BF16),
            VMEM(high.shape, BF16),
            VMEM(fine.shape, BF16),
            VMEM((2 * half, width), BF16),
            VMEM((tiles, share, tile), F32),
            VMEM((tiles, share, tile), F32),
            VMEM((tiles, tile, share), F32),
            pltpu.SemaphoreType.DMA((tiles, 3)),
            pltpu.SemaphoreType.DMA((7,)),
        ],
        compiler_params=params(24 if parts <= 4 else 60),
        cost_estimate=cost(6 * parts * rows * share * hidden_units, 12 * share * hidden_units),
        name="final",
    )(*in_hbm(received[0], own_acts, high, fine), back, low, arrived, w_shares, *received[1:])


def grads_kernel(capacity, hit_ref, *refs):
    pairs, (low_ref, high_ref) = refs[:-2], refs[-2:]
    rows = jnp.concatenate(
        [joined(pairs[i], pairs[i + 1], capacity) for i in range(0, len(pairs), 2)], axis=0
    )
    across = (((0,), (0,)), ((), ()))
    total = lax.dot_general(hit_ref[...], rows, across, preferred_element_type=F32).astype(BF16)
    half = low_ref.shape[0]
    low_ref[...] = total[:half]
    high_ref[...] = total[half:]


def combine_grads(hit, pairs, capacity):
    slots, tok_dev = hit.shape
    flat = [a for p in pairs for a in p]
    width = flat[0].shape[1]
    half = jax.ShapeDtypeStruct((tok_dev // 2, width), BF16)
    return pl.pallas_call(
        functools.partial(grads_kernel, capacity),
        out_shape=[half, half],
        in_specs=[WHOLE] * (1 + len(flat)),
        out_specs=[WHOLE, WHOLE],
        compiler_params=params(12),
        cost_estimate=cost(2 * slots * tok_dev * width, 6 * tok_dev * width),
        name="combine_grads",
    )(hit, *flat)


def send_chips(blocks):
    return [xor_permute(b, "expert", 2 * z) if z else b for z, b in enumerate(blocks)]


def cross(direct, waits=()):
    return [
        (block, xor_permute(after(block, *waits) if z else block, "expert", 1))
        for z, block in enumerate(direct)
    ]


def swapped(array, key):
    ways = [
        functools.partial(xor_permute, axis="dp", key=j) for j in range(1, lax.axis_size("dp"))
    ]
    return lax.switch(key - 1, ways, array)


def spread_acts(sent):
    if lax.axis_size("dp") != 4:
        return [sent[0]] + [xor_permute(sent[j], "dp", j) for j in range(1, len(sent))], []
    acts = sent[1].shape[1] - sent[3].shape[1]
    near = xor_permute(sent[1], "dp", 1)
    side = xor_permute(sent[2], "dp", 2)
    far = xor_permute(sent[3], "dp", 3)
    half = side.shape[0] // 2
    passed = [side[:half], near[half:]]
    halves = [xor_permute(passed[0], "dp", 1), xor_permute(passed[1], "dp", 2)]
    return [sent[0], near, side, far, *halves], passed


def after(value, *others):
    return lax.optimization_barrier((value, *others))[0] if others else value


def all_to_all(array, axis):
    return lax.all_to_all(array, axis, split_axis=0, concat_axis=0, tiled=True)


def per_device(
    tokens,
    cotangent,
    w_gate,
    w_up,
    w_down,
    slot_rows,
    slot_counts,
    slot_gates,
    seq_lengths,
    matching,
):
    capacity = slot_rows.shape[2]
    key = matching[0, 0]
    moved, low, weighted, hit, high, fine = prepare(
        slot_rows, slot_gates, slot_counts, seq_lengths, tokens, cotangent
    )
    weighted = weighted.reshape(slot_rows.shape[1], capacity, tokens.shape[1])
    weighted = all_to_all(weighted, "expert")
    picked = pick(hit, low, swapped(moved, key), capacity)
    x_direct = send_chips(picked)
    w_rows, w_shares = gather_rows(weighted)
    w_shares = all_to_all(w_shares, "dp")
    x_pairs = cross(x_direct, [w_rows])
    token_rows, expert_out, sent = expert(x_pairs, w_rows, w_gate, w_up, w_down, capacity)
    tok_pairs = cross(send_chips(token_rows))
    received, early = spread_acts(sent)
    back = all_to_all(after(expert_out, w_shares, *[p[0] for p in tok_pairs]), "expert")
    low_grads, high_grads = combine_grads(hit, tok_pairs, capacity)
    return tuple(
        final(
            high, fine, back, low_grads, swapped(high_grads, key), w_shares, sent[1], received
        )
    )


def solution(mesh):
    return jax.shard_map(
        per_device,
        mesh=mesh,
        in_specs=(
            P(("dp", "expert"), None),
            P(("dp", "expert"), None),
            P("expert", None, None),
            P("expert", None, None),
            P("expert", None, None),
            P(("dp", "expert"), None, None),
            P(("dp", "expert"), None),
            P(("dp", "expert"), None, None),
            P(("dp", "expert"), None),
            P("expert", None),
        ),
        out_specs=(
            P(("dp", "expert"), None),
            P(("dp", "expert"), None),
            P("expert", "dp", None),
            P("expert", "dp", None),
            P("expert", None, "dp"),
        ),
        check_vma=False,
    )
```

```python
import functools

import jax
import jax.numpy as jnp
from jax import lax
from jax.experimental import pallas as pl
from jax.experimental.pallas import tpu as pltpu
from jax.sharding import PartitionSpec as P

F32 = jnp.float32
BF16 = jnp.bfloat16
VMEM = pltpu.VMEM
WHOLE = pl.BlockSpec(memory_space=pltpu.VMEM)
TILE = 256
PIECES = 4
MIB = 1024 * 1024


def params(mib):
    return pltpu.CompilerParams(vmem_limit_bytes=mib * MIB)


def in_hbm(*arrays):
    return [pltpu.with_memory_space_constraint(a, pltpu.HBM) for a in arrays]


def cost(flops, bytes_accessed):
    return pl.CostEstimate(flops=int(flops), bytes_accessed=int(bytes_accessed), transcendentals=0)


def xor_permute(array, axis, key):
    size = lax.axis_size(axis)
    return lax.ppermute(array, axis, [(i, i ^ key) for i in range(size)])


def column_of(row, length):
    diagonal = lax.broadcasted_iota(jnp.int32, (length, length), 0) == lax.broadcasted_iota(
        jnp.int32, (length, length), 1
    )
    spread = jnp.where(diagonal, jnp.broadcast_to(row.astype(F32), (length, length)), 0.0)
    return jnp.sum(spread, axis=1, keepdims=True)


def table_columns(table, order):
    return jnp.concatenate([column_of(row, row.shape[1]) for row in (table(e) for e in order)], axis=0)


def keep_valid(values, lengths, first_slot, slot_len):
    rows = lax.broadcasted_iota(jnp.int32, values.shape, 0)
    limit = jnp.zeros(values.shape, jnp.int32)
    for slot in range(values.shape[0] // slot_len):
        used = lengths[:, first_slot + slot : first_slot + slot + 1]
        limit = jnp.where(rows // slot_len == slot, slot * slot_len + used, limit)
    return jnp.where(rows < limit, values.astype(F32), 0.0).astype(values.dtype)


def prepare_kernel(sizes, *refs):
    window, capacity, tok_dev, slot_len = sizes
    sources, outs, held = refs[:6], refs[6:12], refs[12:18]
    high_held, fine_held, weighted_held, sems, out_sems = refs[18:]
    copies = [
        pltpu.make_async_copy(source, place, sems.at[i])
        for i, (source, place) in enumerate(zip(sources, held))
    ]
    for i in (0, 1, 2, 5, 3, 4):
        copies[i].start()
    rows_ref, gates_ref, counts_ref, lengths_ref, tok_ref, cot_ref = held
    moved_ref, low_ref, weighted_ref, hit_ref, high_ref, fine_ref = outs
    me = lax.axis_index("expert")
    half = tok_dev // 2
    pair = 2 * capacity
    for i in (0, 1, 2, 5):
        copies[i].wait()

    def gate_of(e):
        slot = lax.broadcasted_iota(jnp.int32, (1, capacity), 1)
        owner = lax.broadcasted_iota(jnp.int32, (1, window), 1) == e
        count = jnp.sum(jnp.where(owner, counts_ref[...].astype(F32), 0.0), axis=1, keepdims=True)
        return jnp.where(slot.astype(F32) < count, gates_ref[0, pl.ds(e, 1), :], 0.0)

    order = [me ^ d for d in range(window)]
    gate = table_columns(gate_of, order)
    index = table_columns(lambda e: rows_ref[0, pl.ds(e, 1), :], order).astype(jnp.int32)
    hit = lax.broadcasted_iota(jnp.int32, (window * capacity, tok_dev), 1) == index
    picked = jnp.dot(hit.astype(BF16), cot_ref[...], preferred_element_type=F32)
    weighted = gate * picked
    swapped_cores = me % 2 == 1
    for z in range(window // 2):
        one = weighted[z * pair : z * pair + capacity]
        other = weighted[z * pair + capacity : (z + 1) * pair]
        block = jnp.where(
            swapped_cores,
            jnp.concatenate([other, one], axis=0),
            jnp.concatenate([one, other], axis=0),
        )
        weighted_held[(me // 2) ^ z] = block.astype(BF16)
    hit_ref[...] = hit.astype(BF16)
    table = jnp.where(hit, jnp.broadcast_to(gate, hit.shape), 0.0)
    high = table.astype(BF16)
    high_held[...] = high
    fine_held[...] = (table - high.astype(F32)).astype(BF16)
    stores = [
        pltpu.make_async_copy(a, b, out_sems.at[i])
        for i, (a, b) in enumerate(
            ((weighted_held, weighted_ref), (high_held, high_ref), (fine_held, fine_ref))
        )
    ]
    for copy in stores:
        copy.start()
    for i in (3, 4):
        copies[i].wait()
    lengths = lengths_ref[...]
    moved_ref[...] = keep_valid(tok_ref[half:, :], lengths, half // slot_len, slot_len)
    low_ref[...] = keep_valid(tok_ref[:half, :], lengths, 0, slot_len)
    for copy in stores:
        copy.wait()


def prepare(slot_rows, slot_gates, slot_counts, seq_lengths, tokens, cotangent):
    tok_dev, width = tokens.shape
    window, capacity = slot_rows.shape[1:]
    half = tok_dev // 2
    slot_len = tok_dev // seq_lengths.shape[1]
    sources = (slot_rows, slot_gates, slot_counts, seq_lengths, tokens, cotangent)
    table = jax.ShapeDtypeStruct((window * capacity, tok_dev), BF16)
    return pl.pallas_call(
        functools.partial(prepare_kernel, (window, capacity, tok_dev, slot_len)),
        out_shape=[
            jax.ShapeDtypeStruct((half, width), BF16),
            jax.ShapeDtypeStruct((half, width), BF16),
            pltpu.HBM((window // 2, 2 * capacity, width), BF16),
            table,
            pltpu.HBM(table.shape, table.dtype),
            pltpu.HBM(table.shape, table.dtype),
        ],
        in_specs=[pl.BlockSpec(memory_space=pltpu.HBM)] * len(sources),
        out_specs=[WHOLE] * 2
        + [pl.BlockSpec(memory_space=pltpu.HBM), WHOLE]
        + [pl.BlockSpec(memory_space=pltpu.HBM)] * 2,
        scratch_shapes=[VMEM(a.shape, a.dtype) for a in sources]
        + [VMEM(table.shape, BF16)] * 2
        + [VMEM((window // 2, 2 * capacity, width), BF16)]
        + [pltpu.SemaphoreType.DMA((len(sources),)), pltpu.SemaphoreType.DMA((3,))],
        compiler_params=params(12),
        cost_estimate=cost(2 * window * capacity * tok_dev * width, 5 * tok_dev * width),
        name="prepare",
    )(*in_hbm(*sources))


def pick_kernel(pair, hit_ref, low_ref, arrived_ref, *outs):
    shuffled = jnp.concatenate([low_ref[...], arrived_ref[...]], axis=0)
    picked = jnp.dot(hit_ref[...], shuffled, preferred_element_type=F32).astype(BF16)
    for z, out in enumerate(outs):
        out[...] = picked[z * pair : (z + 1) * pair]


def pick(hit, low, arrived, capacity):
    pair, width = 2 * capacity, low.shape[1]
    slots, tok_dev = hit.shape
    return pl.pallas_call(
        functools.partial(pick_kernel, pair),
        out_shape=[jax.ShapeDtypeStruct((pair, width), BF16)] * (slots // pair),
        in_specs=[WHOLE] * 3,
        out_specs=[WHOLE] * (slots // pair),
        compiler_params=params(8),
        cost_estimate=cost(2 * slots * tok_dev * width, 5 * tok_dev * width),
        name="pick",
    )(hit, low, arrived)


def joined(direct, crossed, capacity, columns=slice(None)):
    one, other = direct[:, columns].astype(F32), crossed[:, columns].astype(F32)
    rows = lax.broadcasted_iota(jnp.int32, one.shape, 0)
    return jnp.where(rows < capacity, one, other).astype(BF16)


def share_columns(rows, outs):
    me = lax.axis_index("dp")
    share = outs[1].shape[1]
    for j, out in enumerate(outs):
        if out is None:
            continue
        out[...] = rows[:, pl.ds(pl.multiple_of((me ^ j) * share, share), share)]


def gather_kernel(weighted_ref, rows_ref, shares_ref):
    me = lax.axis_index("expert")
    window, capacity, _ = weighted_ref.shape
    pair = 2 * capacity
    for z in range(window // 2):
        both = [weighted_ref[me ^ (2 * z + core)].astype(F32) for core in range(2)]
        rows_ref[z * pair : (z + 1) * pair, :] = jnp.concatenate(both, axis=0).astype(BF16)
    share = shares_ref.shape[2]
    for g in range(shares_ref.shape[0]):
        shares_ref[g] = rows_ref[:, g * share : (g + 1) * share]


def gather_rows(weighted):
    window, capacity, width = weighted.shape
    rows = window * capacity
    replicas = lax.axis_size("dp")
    return pl.pallas_call(
        gather_kernel,
        out_shape=[
            jax.ShapeDtypeStruct((rows, width), BF16),
            jax.ShapeDtypeStruct((replicas, rows, width // replicas), BF16),
        ],
        in_specs=[WHOLE],
        out_specs=[WHOLE] * 2,
        compiler_params=params(12),
        cost_estimate=cost(0, 8 * rows * width),
        name="gather_rows",
    )(weighted)


def expert_kernel(sizes, *refs):
    count, capacity, tile, replicas = sizes
    x_refs, w_ref, weights = refs[: 2 * count], refs[2 * count], refs[2 * count + 1 : 2 * count + 4]
    tok_refs = refs[2 * count + 4 : 3 * count + 4]
    out_ref, sent_refs = refs[3 * count + 4], refs[3 * count + 5 : 3 * count + 5 + replicas]
    x_all, hid_all, gg_all, gu_all, pre_gate, grad_hidden, *held, sems = refs[
        3 * count + 5 + replicas :
    ]
    wide_count = sum(ref.shape[1] > sent_refs[0].shape[1] for ref in sent_refs)
    sent_held, held = held[3:], held[:3]
    sent_copies = [
        pltpu.make_async_copy(a, b, sems.at[3, 1 + i])
        for i, (a, b) in enumerate(zip(sent_held, sent_refs[1 : 1 + wide_count]))
    ]
    sent_refs = [sent_refs[0], *sent_held, *sent_refs[1 + wide_count :]]
    gate_ref, up_ref, down_ref = held
    copies = []
    for i, (source, place) in enumerate(zip(weights, held)):
        part = source.shape[1] // PIECES
        pieces = [pl.ds(k * part, part) for k in range(PIECES)]
        copies.append(
            [
                pltpu.make_async_copy(source.at[:, rows, :], place.at[:, rows, :], sems.at[i, k])
                for k, rows in enumerate(pieces)
            ]
        )
    for copy in copies[0] + copies[2]:
        copy.start()
    me = lax.axis_index("expert")
    pair = 2 * capacity
    width = x_all.shape[1]
    share = width // replicas
    turned = (((1,), (1,)), ((), ()))
    for z in range(count):
        x_all[z * pair : (z + 1) * pair, :] = joined(x_refs[2 * z], x_refs[2 * z + 1], capacity)
    own = pl.ds(pl.multiple_of(lax.axis_index("dp") * share, share), share)
    own_copy = pltpu.make_async_copy(x_all.at[:, own], sent_refs[0], sems.at[3, 0])
    own_copy.start()
    share_columns(x_all, [None] + [s.at[:, s.shape[1] - share :] for s in sent_refs[1:]])
    spans = [slice(f * tile, (f + 1) * tile) for f in range(hid_all.shape[1] // tile)]
    for copy in copies[0]:
        copy.wait()
    for copy in copies[1]:
        copy.start()
    for span in spans:
        pre_gate[:, span] = jnp.dot(x_all[...], gate_ref[0, :, span], preferred_element_type=F32)
    for copy in copies[2]:
        copy.wait()
    for span in spans:
        grad_hidden[:, span] = lax.dot_general(
            w_ref[...], down_ref[0, span, :], turned, preferred_element_type=F32
        )
    for copy in copies[1]:
        copy.wait()
    for f, span in enumerate(spans):
        gate, grad = pre_gate[:, span], grad_hidden[:, span]
        pre_up = jnp.dot(x_all[...], up_ref[0, :, span], preferred_element_type=F32)
        sig = jax.nn.sigmoid(gate)
        silu = gate * sig
        hid_all[:, span] = (silu * pre_up).astype(BF16)
        gg_all[:, span] = (grad * pre_up * sig * (1.0 + gate * (1.0 - sig))).astype(BF16)
        gu_all[:, span] = (grad * silu).astype(BF16)
        for sent in sent_refs[1:]:
            if sent.shape[1] > share:
                for k, source in enumerate((hid_all, gg_all, gu_all)):
                    sent[:, (3 * f + k) * tile : (3 * f + k + 1) * tile] = source[:, span]
    for copy in sent_copies:
        copy.start()
    wide = 2 * tile
    for n in range(width // wide):
        span = slice(n * wide, (n + 1) * wide)
        tok = lax.dot_general(
            gg_all[...], gate_ref[0, span, :], turned, preferred_element_type=F32
        ) + lax.dot_general(gu_all[...], up_ref[0, span, :], turned, preferred_element_type=F32)
        tok = tok.astype(BF16)
        out = jnp.dot(hid_all[...], down_ref[0, :, span], preferred_element_type=F32)
        swapped_cores = me % 2 == 1
        for z in range(count):
            tok_refs[z][:, span] = tok[z * pair : (z + 1) * pair]
        for z in range(count):
            one = out[z * pair : z * pair + capacity]
            other = out[z * pair + capacity : (z + 1) * pair]
            block = jnp.where(
                swapped_cores,
                jnp.concatenate([other, one], axis=0),
                jnp.concatenate([one, other], axis=0),
            )
            out_ref[(me // 2) ^ z, :, span] = block.astype(BF16)
    for copy in [own_copy, *sent_copies]:
        copy.wait()


def expert(x_pairs, w_rows, w_gate, w_up, w_down, capacity):
    count = len(x_pairs)
    flat = [a for p in x_pairs for a in p]
    pair, width = flat[0].shape
    hidden_units = w_gate.shape[2]
    rows = count * pair
    replicas = lax.axis_size("dp")
    share = width // replicas
    block = jax.ShapeDtypeStruct((pair, width), BF16)
    sent = [jax.ShapeDtypeStruct((rows, 3 * hidden_units + share), BF16)] * replicas
    if replicas == 4:
        sent[3] = jax.ShapeDtypeStruct((rows, share), BF16)
    sent[0] = pltpu.HBM((rows, share), BF16)
    large = [a for a in sent[1:] if a.shape[1] > share]
    sent[1 : 1 + len(large)] = [pltpu.HBM(a.shape, BF16) for a in large]
    results = pl.pallas_call(
        functools.partial(expert_kernel, (count, capacity, TILE, replicas)),
        out_shape=[block] * count
        + [jax.ShapeDtypeStruct((count, pair, width), BF16)]
        + sent,
        in_specs=[WHOLE] * (2 * count + 1) + [pl.BlockSpec(memory_space=pltpu.HBM)] * 3,
        out_specs=[WHOLE] * (count + 1)
        + [pl.BlockSpec(memory_space=pltpu.HBM)] * (1 + len(large))
        + [WHOLE] * (replicas - 1 - len(large)),
        scratch_shapes=[VMEM((rows, width), BF16)]
        + [VMEM((rows, hidden_units), BF16)] * 3
        + [VMEM((rows, hidden_units), F32)] * 2
        + [VMEM(a.shape, BF16) for a in (w_gate, w_up, w_down, *large)]
        + [pltpu.SemaphoreType.DMA((4, max(PIECES, 1 + len(large))))],
        compiler_params=params(32 if replicas <= 4 else 56),
        cost_estimate=cost(
            12 * rows * width * hidden_units, 6 * width * hidden_units + 10 * rows * width
        ),
        name="expert",
    )(*flat, w_rows, *in_hbm(w_gate, w_up, w_down))
    return (
        results[:count],
        results[count].reshape(2 * count, capacity, width),
        results[count + 1 :],
    )


def final_kernel(sizes, *refs):
    share, tile, parts = sizes
    loads, refs = list(refs[:4]), refs[4:]
    back_ref, low_ref, arrived_ref, w_ref, refs = *refs[:4], refs[4:]
    sources, outs, scratch = refs[:-15], refs[-15:-10], refs[-10:]
    own_share, own_acts, high_ref, fine_ref, out_held, *held, sems, side_sems = scratch
    loads = [
        pltpu.make_async_copy(a, b, side_sems.at[i])
        for i, (a, b) in enumerate(zip(loads, (own_share, own_acts, high_ref, fine_ref)))
    ]
    half = low_ref.shape[0]
    stores = [
        pltpu.make_async_copy(low_ref, outs[1].at[:half], side_sems.at[4]),
        pltpu.make_async_copy(arrived_ref, outs[1].at[half:], side_sems.at[5]),
    ]
    for copy in loads + stores:
        copy.start()
    for copy in loads[:2]:
        copy.wait()
    sources = [own_share, *sources]
    me = lax.axis_index("dp")
    acts_width = own_acts.shape[1] - share
    across = (((0,), (0,)), ((), ()))
    x = jnp.concatenate([r[:, r.shape[1] - share :] for r in sources[:parts]], axis=0)
    w = jnp.concatenate([w_ref[me ^ j] for j in range(parts)], axis=0)
    acts = [own_acts] + [r for r in sources if r.shape[1] > share]
    for f in range(acts_width // (3 * tile)):
        hidden, grad_gate, grad_up = [
            jnp.concatenate(
                [a[:, (3 * f + k) * tile : (3 * f + k + 1) * tile] for a in acts], axis=0
            )
            for k in range(3)
        ]
        span = pl.ds(f * tile, tile)
        gate_held, up_held, down_held = [h.at[f] for h in held]
        gate_held[...] = lax.dot_general(x, grad_gate, across, preferred_element_type=F32)
        up_held[...] = lax.dot_general(x, grad_up, across, preferred_element_type=F32)
        down_held[...] = lax.dot_general(hidden, w, across, preferred_element_type=F32)
        pieces = [
            (gate_held, outs[2].at[0, :, span]),
            (up_held, outs[3].at[0, :, span]),
            (down_held, outs[4].at[0, span, :]),
        ]
        for i, (a, b) in enumerate(pieces):
            copy = pltpu.make_async_copy(a, b, sems.at[f, i])
            copy.start()
            stores.append(copy)
    for copy in loads[2:]:
        copy.wait()
    expert_id = lax.axis_index("expert")
    rows = jnp.concatenate(
        [back_ref[expert_id ^ d].astype(F32) for d in range(back_ref.shape[0])], axis=0
    ).astype(BF16)
    total = lax.dot_general(high_ref[...], rows, across, preferred_element_type=F32)
    total += lax.dot_general(fine_ref[...], rows, across, preferred_element_type=F32)
    out_held[...] = total.astype(BF16)
    stores.append(pltpu.make_async_copy(out_held, outs[0], side_sems.at[6]))
    stores[-1].start()
    for copy in stores:
        copy.wait()


def final(high, fine, back, low, arrived, w_shares, own_acts, received):
    parts, rows, share = w_shares.shape
    half, width = low.shape
    hidden_units = (own_acts.shape[1] - share) // 3
    tile = TILE
    tiles = hidden_units // tile
    hbm = pl.BlockSpec(memory_space=pltpu.HBM)
    return pl.pallas_call(
        functools.partial(final_kernel, (share, tile, parts)),
        out_shape=[
            jax.ShapeDtypeStruct((2 * half, width), BF16),
            jax.ShapeDtypeStruct((2 * half, width), BF16),
            jax.ShapeDtypeStruct((1, share, hidden_units), F32),
            jax.ShapeDtypeStruct((1, share, hidden_units), F32),
            jax.ShapeDtypeStruct((1, hidden_units, share), F32),
        ],
        in_specs=[hbm] * 4 + [WHOLE] * (3 + len(received)),
        out_specs=[hbm] * 5,
        scratch_shapes=[
            VMEM(received[0].shape, BF16),
            VMEM(own_acts.shape, BF16),
            VMEM(high.shape, BF16),
            VMEM(fine.shape, BF16),
            VMEM((2 * half, width), BF16),
            VMEM((tiles, share, tile), F32),
            VMEM((tiles, share, tile), F32),
            VMEM((tiles, tile, share), F32),
            pltpu.SemaphoreType.DMA((tiles, 3)),
            pltpu.SemaphoreType.DMA((7,)),
        ],
        compiler_params=params(24 if parts <= 4 else 60),
        cost_estimate=cost(6 * parts * rows * share * hidden_units, 12 * share * hidden_units),
        name="final",
    )(*in_hbm(received[0], own_acts, high, fine), back, low, arrived, w_shares, *received[1:])


def grads_kernel(capacity, hit_ref, *refs):
    pairs, (low_ref, high_ref) = refs[:-2], refs[-2:]
    rows = jnp.concatenate(
        [joined(pairs[i], pairs[i + 1], capacity) for i in range(0, len(pairs), 2)], axis=0
    )
    across = (((0,), (0,)), ((), ()))
    total = lax.dot_general(hit_ref[...], rows, across, preferred_element_type=F32).astype(BF16)
    half = low_ref.shape[0]
    low_ref[...] = total[:half]
    high_ref[...] = total[half:]


def combine_grads(hit, pairs, capacity):
    slots, tok_dev = hit.shape
    flat = [a for p in pairs for a in p]
    width = flat[0].shape[1]
    half = jax.ShapeDtypeStruct((tok_dev // 2, width), BF16)
    return pl.pallas_call(
        functools.partial(grads_kernel, capacity),
        out_shape=[half, half],
        in_specs=[WHOLE] * (1 + len(flat)),
        out_specs=[WHOLE, WHOLE],
        compiler_params=params(12),
        cost_estimate=cost(2 * slots * tok_dev * width, 6 * tok_dev * width),
        name="combine_grads",
    )(hit, *flat)


def send_chips(blocks):
    return [xor_permute(b, "expert", 2 * z) if z else b for z, b in enumerate(blocks)]


def cross(direct, waits=()):
    return [
        (block, xor_permute(after(block, *waits) if z else block, "expert", 1))
        for z, block in enumerate(direct)
    ]


def swapped(array, key):
    ways = [
        functools.partial(xor_permute, axis="dp", key=j) for j in range(1, lax.axis_size("dp"))
    ]
    return lax.switch(key - 1, ways, array)


def pass_kernel(part, array_ref, out_ref):
    half, acts = out_ref.shape
    out_ref[...] = array_ref[part * half : (part + 1) * half, :acts]


def pass_on(array, acts, part):
    half = jax.ShapeDtypeStruct((array.shape[0] // 2, acts), BF16)
    return pl.pallas_call(
        functools.partial(pass_kernel, part),
        out_shape=half,
        in_specs=[WHOLE],
        out_specs=WHOLE,
        compiler_params=params(8),
        cost_estimate=cost(0, 4 * half.size),
        name="pass_on",
    )(array)


def spread_acts(sent):
    if lax.axis_size("dp") != 4:
        return [sent[0]] + [xor_permute(sent[j], "dp", j) for j in range(1, len(sent))], []
    acts = sent[1].shape[1] - sent[3].shape[1]
    near = xor_permute(sent[1], "dp", 1)
    side = xor_permute(sent[2], "dp", 2)
    far = xor_permute(sent[3], "dp", 3)
    half = side.shape[0] // 2
    acts = sent[1].shape[1] - sent[3].shape[1]
    passed = [pass_on(side, acts, 0), pass_on(near, acts, 1)]
    halves = [xor_permute(passed[0], "dp", 1), xor_permute(passed[1], "dp", 2)]
    return [sent[0], near, side, far, *halves], passed


def after(value, *others):
    return lax.optimization_barrier((value, *others))[0] if others else value


def all_to_all(array, axis):
    return lax.all_to_all(array, axis, split_axis=0, concat_axis=0, tiled=True)


def per_device(
    tokens,
    cotangent,
    w_gate,
    w_up,
    w_down,
    slot_rows,
    slot_counts,
    slot_gates,
    seq_lengths,
    matching,
):
    capacity = slot_rows.shape[2]
    key = matching[0, 0]
    moved, low, weighted, hit, high, fine = prepare(
        slot_rows, slot_gates, slot_counts, seq_lengths, tokens, cotangent
    )
    weighted = weighted.reshape(slot_rows.shape[1], capacity, tokens.shape[1])
    weighted = all_to_all(weighted, "expert")
    picked = pick(hit, low, swapped(moved, key), capacity)
    x_direct = send_chips(picked)
    w_rows, w_shares = gather_rows(weighted)
    w_shares = all_to_all(w_shares, "dp")
    x_pairs = cross(x_direct, [w_rows])
    token_rows, expert_out, sent = expert(x_pairs, w_rows, w_gate, w_up, w_down, capacity)
    tok_pairs = cross(send_chips(token_rows))
    received, early = spread_acts(sent)
    back = all_to_all(after(expert_out, w_shares, *[p[0] for p in tok_pairs]), "expert")
    low_grads, high_grads = combine_grads(hit, tok_pairs, capacity)
    return tuple(
        final(
            high, fine, back, low_grads, swapped(high_grads, key), w_shares, sent[1], received
        )
    )


def solution(mesh):
    return jax.shard_map(
        per_device,
        mesh=mesh,
        in_specs=(
            P(("dp", "expert"), None),
            P(("dp", "expert"), None),
            P("expert", None, None),
            P("expert", None, None),
            P("expert", None, None),
            P(("dp", "expert"), None, None),
            P(("dp", "expert"), None),
            P(("dp", "expert"), None, None),
            P(("dp", "expert"), None),
            P("expert", None),
        ),
        out_specs=(
            P(("dp", "expert"), None),
            P(("dp", "expert"), None),
            P("expert", "dp", None),
            P("expert", "dp", None),
            P("expert", None, "dp"),
        ),
        check_vma=False,
    )
```
